512 devices in a mesh: row: 16 (over z, core), col: 32 (over x, y).
Axes of the slice: x: 4, y: 8, z: 8, core: 2. Of those that a mesh axis runs over, the one named last changes fastest.
Arguments:
- inputs: bfloat16 [1536, 6144], P('col', 'row'), may hold values from -6 to 6
- cotangent: bfloat16 [1536, 6144], P('col', 'row'), may hold values from -4 to 4
- gate_pre: bfloat16 [1536, 16384], P('row', 'col'), may hold values from -10 to 10
- up_pre: bfloat16 [1536, 16384], P('row', 'col'), may hold values from -6 to 6
- gate_weight: bfloat16 [6144, 16384], P('row', 'col'), may hold values from -0.078125 to 0.078125
- up_weight: bfloat16 [6144, 16384], P('row', 'col'), may hold values from -0.078125 to 0.078125
- down_weight: bfloat16 [16384, 6144], P('col', 'row'), may hold values from -0.046875 to 0.046875
Outputs:
- input_grad: bfloat16 [1536, 6144], P('col', 'row')
- gate_grad: bfloat16 [6144, 16384], P('row', 'col')
- up_grad: bfloat16 [6144, 16384], P('row', 'col')
- down_grad: bfloat16 [16384, 6144], P('col', 'row')
The draws below stay inside these ranges and needn't reach their ends.
All inputs are finite; a program needn't handle non-finite values.
Results may differ from the reference program's by a relative error of at most 0.033.
Values may be sent and summed in bfloat16 or wider, within the bound.
A program may use at most 64 MiB of HBM per device.

```python
import jax
import jax.numpy as jnp
from jax import lax

D = 6144
FF = 16384
TOKENS = 1536
N_ROW = 16
N_COL = 32


def steps_of(own_key, shape, pieces, smallest, high):
    loudness, own = 1.0, jax.random.fold_in(own_key, 6)
    for position, parts in pieces:
        heights = jnp.exp(jax.random.uniform(jax.random.fold_in(own, position), (parts,), jnp.float32, smallest / len(pieces), high / len(pieces)))
        loudness = loudness * jnp.repeat(heights, shape[position] // parts).reshape([-1 if axis == position else 1 for axis in range(len(shape))])
    return loudness


def bell_draw(rng, shape, spread, reach, pieces=(), held_as=jnp.bfloat16):
    loudness = steps_of(rng, shape, pieces, -0.22, 0.18) if pieces else 1.0
    entries = jax.random.normal(rng, shape, jnp.float32) * spread * loudness
    return jnp.minimum(jnp.maximum(entries, -reach), reach).astype(held_as)


def setup_inputs(seed: int = 0) -> dict:
    arg_keys = jax.random.split(jax.random.key(seed), 8)
    return {
        "inputs": bell_draw(arg_keys[0], (TOKENS, D), 1.0, 6.0, ((0, 32), (1, 16))),
        "cotangent": bell_draw(arg_keys[1], (TOKENS, D), 0.5, 4.0, ((0, 32), (1, 16))),
        "gate_pre": bell_draw(arg_keys[2], (TOKENS, FF), 2.0, 10.0, ((0, 16), (1, 32))),
        "up_pre": bell_draw(arg_keys[3], (TOKENS, FF), 1.0, 6.0, ((0, 16), (1, 32))),
        "gate_weight": bell_draw(arg_keys[4], (D, FF), D ** -0.5, 0.078125, ((0, 16), (1, 32))),
        "up_weight": bell_draw(arg_keys[5], (D, FF), D ** -0.5, 0.078125, ((0, 16), (1, 32))),
        "down_weight": bell_draw(arg_keys[6], (FF, D), FF ** -0.5, 0.046875, ((0, 32), (1, 16))),
    }


def reference(inputs, cotangent, gate_pre, up_pre, gate_weight, up_weight, down_weight):
    gate_value = gate_pre.astype(jnp.float32)
    up_value = up_pre.astype(jnp.float32)
    sigma = jax.nn.sigmoid(gate_value)
    silu_value = gate_value * sigma
    hidden = (silu_value * up_value).astype(jnp.bfloat16)

    feat_block = D // N_ROW

    def add_feature_block(total, index):
        start = (index * feat_block).astype(jnp.int32)
        cot_block = lax.dynamic_slice_in_dim(cotangent, start, feat_block, 1)
        down_block = lax.dynamic_slice_in_dim(down_weight, start, feat_block, 1)
        partial_sum = jnp.dot(cot_block, down_block.T, preferred_element_type=jnp.float32)
        return total + partial_sum.astype(jnp.bfloat16).astype(jnp.float32), None

    hidden_grad, _ = lax.scan(add_feature_block, jnp.zeros((TOKENS, FF), jnp.float32), jnp.arange(N_ROW, dtype=jnp.int32))

    gate_delta = (hidden_grad * up_value * sigma * (1.0 + gate_value * (1.0 - sigma))).astype(jnp.bfloat16)
    up_delta = (hidden_grad * silu_value).astype(jnp.bfloat16)
    down_grad = jnp.dot(hidden.T, cotangent, preferred_element_type=jnp.float32).astype(jnp.bfloat16)
    gate_grad = jnp.dot(inputs.T, gate_delta, preferred_element_type=jnp.float32).astype(jnp.bfloat16)
    up_grad = jnp.dot(inputs.T, up_delta, preferred_element_type=jnp.float32).astype(jnp.bfloat16)

    unit_block = FF // N_COL

    def add_unit_block(total, index):
        start = (index * unit_block).astype(jnp.int32)
        gate_part = lax.dynamic_slice_in_dim(gate_delta, start, unit_block, 1)
        up_part = lax.dynamic_slice_in_dim(up_delta, start, unit_block, 1)
        gate_w = lax.dynamic_slice_in_dim(gate_weight, start, unit_block, 1)
        up_w = lax.dynamic_slice_in_dim(up_weight, start, unit_block, 1)
        term = jnp.dot(gate_part, gate_w.T, preferred_element_type=jnp.float32)
        term = term + jnp.dot(up_part, up_w.T, preferred_element_type=jnp.float32)
        return total + term.astype(jnp.bfloat16).astype(jnp.float32), None

    input_sum, _ = lax.scan(add_unit_block, jnp.zeros((TOKENS, D), jnp.float32), jnp.arange(N_COL, dtype=jnp.int32))
    input_grad = input_sum.astype(jnp.bfloat16)
    return input_grad, gate_grad, up_grad, down_grad
```

```python
import functools

import jax
import jax.numpy as jnp
from jax import lax
from jax.experimental import pallas as pl
from jax.experimental.pallas import tpu as pltpu
from jax.sharding import PartitionSpec as P

MESH = pl.DeviceIdType.MESH
BF16 = jnp.bfloat16
F32 = jnp.float32

N_X, N_Y, N_Z = 4, 8, 8
TOK = 48
D_OWN = 384
D_CHIP = 768
F_OWN = 512
N_SEMS = 128


def nt_dot(left, right):
    return lax.dot_general(left, right, (((1,), (1,)), ((), ())), preferred_element_type=F32)


def nn_dot(left, right):
    return lax.dot_general(left, right, (((1,), (0,)), ((), ())), preferred_element_type=F32)


def tn_dot(left, right):
    return lax.dot_general(left, right, (((0,), (0,)), ((), ())), preferred_element_type=F32)


def kernel(
    inp_in, cot_in, gate_in, up_in, wg_in, wu_in, wd_in,
    ig_out, gg_out, ug_out, dg_out,
    cot_y, inp_y, cot, inp, gate, up, wg, wu, wd,
    part, rs_send, rs_recv, hgrad, lin_g, lin_u, hidden, delta_g, delta_u,
    ig_part, xs_send, xs_recv, ig_own, ig_sib, ig_got, ys_send, ys_recv,
    dg_send, gg_send, ug_send, dg_got, gg_got, ug_got, dg_own, gg_own, ug_own,
    send_sems, recv_sems, local_sems,
):
    row = lax.axis_index("row")
    col = lax.axis_index("col")
    z, core = row // 2, row % 2
    x, y = col // N_Y, col % N_Y

    sib = (z * 2 + 1 - core, col)
    z_dev = {+1: (((z + 1) % N_Z) * 2 + core, col), -1: (((z + N_Z - 1) % N_Z) * 2 + core, col)}
    x_dev = {+1: (row, ((x + 1) % N_X) * N_Y + y), -1: (row, ((x + N_X - 1) % N_X) * N_Y + y)}
    y_dev = {+1: (row, x * N_Y + (y + 1) % N_Y), -1: (row, x * N_Y + (y + N_Y - 1) % N_Y)}

    copies = []

    def send(src, dst, device):
        k = len(copies)
        cp = pltpu.make_async_remote_copy(
            src_ref=src, dst_ref=dst, send_sem=send_sems.at[k], recv_sem=recv_sems.at[k],
            device_id=device, device_id_type=MESH,
        )
        cp.start()
        copies.append(cp)
        return cp

    local = []

    def move(src, dst):
        cp = pltpu.make_async_copy(src, dst, local_sems.at[len(local)])
        cp.start()
        local.append(cp)
        return cp

    def hops(n, long_way):
        return {long_way: n // 2, -long_way: n // 2 - 1}

    class Gather:
        def __init__(self, n, me, devs, long_way, slot, own):
            self.n, self.me, self.devs, self.slot, self.own = n, me, devs, slot, own
            self.hops = hops(n, long_way)
            self.cps = {}

        def start(self, s):
            for way in (+1, -1):
                if s <= self.hops[way]:
                    owner = (self.me - way * (s - 1) + self.n) % self.n
                    src = self.own if s == 1 else self.slot(owner)
                    self.cps[way, s] = send(src, self.slot(owner), self.devs[way])

        def wait(self, s):
            for way in (+1, -1):
                if s <= self.hops[way]:
                    self.cps[way, s].wait_recv()

    class Reduce:
        def __init__(self, n, me, devs, long_way, part, send_slot, recv_slot):
            self.n, self.me, self.devs = n, me, devs
            self.part, self.send_slot, self.recv_slot = part, send_slot, recv_slot
            self.hops = hops(n, long_way)
            self.cps = {}

        def start(self, s):
            for way in (+1, -1):
                last = self.hops[way]
                if s <= last:
                    if s > 1:
                        self.cps[way, s - 1].wait_recv()
                    dest = (self.me + way * (last - s + 1) + self.n) % self.n
                    value = self.part(dest)
                    if s > 1:
                        value = value + self.recv_slot(way, s - 1)[...].astype(F32)
                    out = self.send_slot(way, s)
                    out[...] = value.astype(BF16)
                    self.cps[way, s] = send(out, self.recv_slot(way, s), self.devs[way])

        def result(self):
            total = self.part(self.me)
            for way in (+1, -1):
                last = self.hops[way]
                self.cps[way, last].wait_recv()
                total = total + self.recv_slot(way, last)[...].astype(F32)
            return total

    barrier = pltpu.get_barrier_semaphore()
    for dev in (sib, z_dev[1], z_dev[-1], x_dev[1], x_dev[-1], y_dev[1], y_dev[-1]):
        pl.semaphore_signal(barrier, inc=1, device_id=dev, device_id_type=MESH)
    pl.semaphore_wait(barrier, 7)

    lo, hi = pl.ds(0, D_OWN), pl.ds(D_OWN, D_OWN)

    def y_slot(buf):
        return lambda yy: buf.at[yy // 4, (yy // 2) % 2, yy % 2]

    cot_ring = Gather(N_Y, y, y_dev, +1, y_slot(cot_y), cot_in)
    inp_ring = Gather(N_Y, y, y_dev, -1, y_slot(inp_y), inp_in)
    gate_ring = Gather(N_Z, z, z_dev, +1, lambda zz: gate.at[:, zz], gate_in)
    up_ring = Gather(N_Z, z, z_dev, -1, lambda zz: up.at[:, zz], up_in)

    cot_ring.start(1)
    gate_ring.start(1)
    up_ring.start(1)
    wd_cp = send(wd_in, wd.at[:, hi], sib)
    inp_ring.start(1)
    wg_cp = send(wg_in, wg.at[hi], sib)
    wu_cp = send(wu_in, wu.at[hi], sib)
    cot_self = move(cot_in, y_slot(cot_y)(y))
    inp_self = move(inp_in, y_slot(inp_y)(y))
    gate_self = move(gate_in, gate.at[:, z])
    up_self = move(up_in, up.at[:, z])
    wd_self = move(wd_in, wd.at[:, lo])
    wg_self = move(wg_in, wg.at[lo])
    wu_self = move(wu_in, wu.at[lo])

    for s in (1, 2, 3):
        cot_ring.wait(s)
        cot_ring.start(s + 1)
        inp_ring.wait(s)
        inp_ring.start(s + 1)
        if s == 2:
            gate_ring.wait(1)
            gate_ring.start(2)
            up_ring.wait(1)
            up_ring.start(2)
    cot_ring.wait(4)
    cot_self.wait()

    def halves(buf_y, buf):
        swaps = [send(buf_y.at[:, 1 - core, h], buf.at[h, pl.ds(2 * x, 2), :, hi], sib) for h in (0, 1)]
        moves = [move(buf_y.at[:, core, h], buf.at[h, pl.ds(2 * x, 2), :, lo]) for h in (0, 1)]
        for cp in moves:
            cp.wait()
        for cp in swaps:
            cp.wait_recv()

    def x_slot(buf, h, xx):
        return buf.at[h, pl.ds(2 * xx, 2)]

    def x_start(buf):
        cps = {}
        for h in (0, 1):
            for way in (+1, -1):
                hh = h if way == 1 else 1 - h
                cps[way, hh] = send(x_slot(buf, hh, x), x_slot(buf, hh, x), x_dev[way])
        return cps

    def x_forward(buf, cps):
        fwd = []
        for way, h in ((+1, 0), (-1, 1)):
            cps[way, h].wait_recv()
            owner = (x - way + N_X) % N_X
            fwd.append(send(x_slot(buf, h, owner), x_slot(buf, h, owner), x_dev[way]))
        return fwd

    def x_finish(cps, fwd):
        cps[+1, 1].wait_recv()
        cps[-1, 0].wait_recv()
        for cp in fwd:
            cp.wait_recv()

    halves(cot_y, cot)
    cot_cps = x_start(cot)
    inp_ring.wait(4)
    inp_self.wait()
    halves(inp_y, inp)
    gate_ring.wait(2)
    gate_ring.start(3)
    up_ring.wait(2)
    up_ring.start(3)
    cot_fwd = x_forward(cot, cot_cps)
    gate_ring.wait(3)
    gate_ring.start(4)
    up_ring.wait(3)
    up_ring.start(4)
    wd_self.wait()
    wd_cp.wait_recv()
    x_finish(cot_cps, cot_fwd)
    inp_cps = x_start(inp)

    for h in (0, 1):
        for n in (0, 1):
            cols = pl.ds(n * 256, 256)
            left = cot[h].reshape(8 * TOK, D_CHIP)
            part[h, :, :, cols] = nt_dot(left, wd[cols, :]).reshape(8, TOK, 256)

    red = [
        Reduce(
            N_Z, z, z_dev, +1 if h == 0 else -1,
            lambda zz, h=h: part[h, zz],
            lambda way, s, h=h: rs_send.at[h, (way + 1) // 2, s - 1],
            lambda way, s, h=h: rs_recv.at[h, (way + 1) // 2, s - 1],
        )
        for h in (0, 1)
    ]
    for h in (0, 1):
        red[h].start(1)
    for h in (0, 1):
        red[h].start(2)

    gate_ring.wait(4)
    up_ring.wait(4)
    gate_self.wait()
    up_self.wait()

    def activations(h):
        @pl.loop(0, N_Z)
        def _(zz):
            g = gate[h, zz].astype(F32)
            u = up[h, zz].astype(F32)
            s = 1.0 / (1.0 + jnp.exp(-g))
            silu = g * s
            hidden[h, zz] = (silu * u).astype(BF16)
            lin_g[h, zz] = u * s * (1.0 + g * (1.0 - s))
            lin_u[h, zz] = silu

    activations(0)
    for h in (0, 1):
        red[h].start(3)
    activations(1)
    for h in (0, 1):
        red[h].start(4)

    inp_fwd = x_forward(inp, inp_cps)

    hg_ring = [
        Gather(N_Z, z, z_dev, +1 if h == 0 else -1, lambda zz, h=h: hgrad.at[h, zz], hgrad.at[h, z])
        for h in (0, 1)
    ]
    for h in (0, 1):
        hgrad[h, z] = red[h].result().astype(BF16)
        hg_ring[h].start(1)

    hid_all = hidden.reshape(2 * N_Z * TOK, F_OWN)
    cot_all = cot.reshape(2 * N_Z * TOK, D_CHIP)
    inp_all = inp.reshape(2 * N_Z * TOK, D_CHIP)
    dgl_all = delta_g.reshape(2 * N_Z * TOK, F_OWN)
    dul_all = delta_u.reshape(2 * N_Z * TOK, F_OWN)

    @pl.loop(0, F_OWN // 128)
    def _(i):
        r = pl.ds(pl.multiple_of(i * 128, 128), 128)
        both = tn_dot(hid_all[:, r], cot_all[...])
        dg_own[r, :] = both[:, :D_OWN]
        dg_send[r, :] = both[:, D_OWN:].astype(BF16)

    dg_cp = send(dg_send, dg_got, sib)

    for s in (1, 2, 3):
        for h in (0, 1):
            hg_ring[h].wait(s)
            hg_ring[h].start(s + 1)
    x_finish(inp_cps, inp_fwd)
    wg_self.wait()
    wu_self.wait()
    wg_cp.wait_recv()
    wu_cp.wait_recv()

    def deltas(h):
        @pl.loop(0, N_Z)
        def _(zz):
            hg = hgrad[h, zz].astype(F32)
            delta_g[h, zz] = (hg * lin_g[h, zz]).astype(BF16)
            delta_u[h, zz] = (hg * lin_u[h, zz]).astype(BF16)

    def input_part(h):
        left_g = delta_g[h].reshape(N_Z * TOK, F_OWN)
        left_u = delta_u[h].reshape(N_Z * TOK, F_OWN)

        @pl.loop(0, D_CHIP // 256)
        def _(i):
            n = pl.ds(pl.multiple_of(i * 256, 256), 256)
            term = nt_dot(left_g, wg[n, :]) + nt_dot(left_u, wu[n, :])
            ig_part[h, :, :, n] = term.reshape(N_Z, TOK, 256)

    ig_red = [
        Reduce(
            N_X, x, x_dev, +1 if h == 0 else -1,
            lambda xx, h=h: ig_part[h, pl.ds(2 * xx, 2)],
            lambda way, s, h=h: xs_send.at[h, (way + 1) // 2, s - 1],
            lambda way, s, h=h: xs_recv.at[h, (way + 1) // 2, s - 1],
        )
        for h in (0, 1)
    ]
    for h in (0, 1):
        hg_ring[h].wait(4)
        deltas(h)
        input_part(h)
        ig_red[h].start(1)

    def weight_grad(delta, own, sent):
        @pl.loop(0, D_OWN // 128)
        def _(i):
            r = pl.ds(pl.multiple_of(i * 128, 128), 128)
            own[r, :] = tn_dot(inp_all[:, r], delta[...])
            r2 = pl.ds(pl.multiple_of(D_OWN + i * 128, 128), 128)
            sent[r, :] = tn_dot(inp_all[:, r2], delta[...]).astype(BF16)

    weight_grad(dgl_all, gg_own, gg_send)
    gg_cp = send(gg_send, gg_got, sib)
    for h in (0, 1):
        ig_red[h].start(2)
    weight_grad(dul_all, ug_own, ug_send)
    ug_cp = send(ug_send, ug_got, sib)

    swaps = []
    for h in (0, 1):
        total = ig_red[h].result()
        ig_own[h] = total[:, :, :D_OWN]
        ig_sib[h] = total[:, :, D_OWN:].astype(BF16)
        swaps.append(send(ig_sib.at[h], ig_got.at[h], sib))

    dg_cp.wait_recv()
    dg_out[...] = (dg_own[...] + dg_got[...].astype(F32)).astype(BF16)
    for cp in swaps:
        cp.wait_recv()

    def y_part(yy):
        h, c, k = yy % 2, (yy // 2) % 2, yy // 4
        mine = (c == core).astype(F32)
        return ig_own[h, k] * mine + ig_got[h, k].astype(F32) * (1.0 - mine)

    y_red = Reduce(
        N_Y, y, y_dev, +1, y_part,
        lambda way, s: ys_send.at[(way + 1) // 2, s - 1],
        lambda way, s: ys_recv.at[(way + 1) // 2, s - 1],
    )
    y_red.start(1)
    y_red.start(2)
    gg_cp.wait_recv()
    gg_out[...] = (gg_own[...] + gg_got[...].astype(F32)).astype(BF16)
    y_red.start(3)
    ug_cp.wait_recv()
    ug_out[...] = (ug_own[...] + ug_got[...].astype(F32)).astype(BF16)
    y_red.start(4)
    ig_out[...] = y_red.result().astype(BF16)

    for cp in copies:
        cp.wait_send()


def on_device(inputs, cotangent, gate_pre, up_pre, gate_weight, up_weight, down_weight):
    vmem = pl.BlockSpec(memory_space=pltpu.VMEM)
    shape = jax.ShapeDtypeStruct
    scratch = [
        pltpu.VMEM((2, 2, 2, TOK, D_OWN), BF16),
        pltpu.VMEM((2, 2, 2, TOK, D_OWN), BF16),
        pltpu.VMEM((2, N_Z, TOK, D_CHIP), BF16),
        pltpu.VMEM((2, N_Z, TOK, D_CHIP), BF16),
        pltpu.VMEM((2, N_Z, TOK, F_OWN), BF16),
        pltpu.VMEM((2, N_Z, TOK, F_OWN), BF16),
        pltpu.VMEM((D_CHIP, F_OWN), BF16),
        pltpu.VMEM((D_CHIP, F_OWN), BF16),
        pltpu.VMEM((F_OWN, D_CHIP), BF16),
        pltpu.VMEM((2, N_Z, TOK, F_OWN), F32),
        pltpu.VMEM((2, 2, 4, TOK, F_OWN), BF16),
        pltpu.VMEM((2, 2, 4, TOK, F_OWN), BF16),
        pltpu.VMEM((2, N_Z, TOK, F_OWN), BF16),
        pltpu.VMEM((2, N_Z, TOK, F_OWN), F32),
        pltpu.VMEM((2, N_Z, TOK, F_OWN), F32),
        pltpu.VMEM((2, N_Z, TOK, F_OWN), BF16),
        pltpu.VMEM((2, N_Z, TOK, F_OWN), BF16),
        pltpu.VMEM((2, N_Z, TOK, F_OWN), BF16),
        pltpu.VMEM((2, N_Z, TOK, D_CHIP), F32),
        pltpu.VMEM((2, 2, 2, 2, TOK, D_CHIP), BF16),
        pltpu.VMEM((2, 2, 2, 2, TOK, D_CHIP), BF16),
        pltpu.VMEM((2, 2, TOK, D_OWN), F32),
        pltpu.VMEM((2, 2, TOK, D_OWN), BF16),
        pltpu.VMEM((2, 2, TOK, D_OWN), BF16),
        pltpu.VMEM((2, 4, TOK, D_OWN), BF16),
        pltpu.VMEM((2, 4, TOK, D_OWN), BF16),
        pltpu.VMEM((F_OWN, D_OWN), BF16),
        pltpu.VMEM((D_OWN, F_OWN), BF16),
        pltpu.VMEM((D_OWN, F_OWN), BF16),
        pltpu.VMEM((F_OWN, D_OWN), BF16),
        pltpu.VMEM((D_OWN, F_OWN), BF16),
        pltpu.VMEM((D_OWN, F_OWN), BF16),
        pltpu.VMEM((F_OWN, D_OWN), F32),
        pltpu.VMEM((D_OWN, F_OWN), F32),
        pltpu.VMEM((D_OWN, F_OWN), F32),
        pltpu.SemaphoreType.DMA((N_SEMS,)),
        pltpu.SemaphoreType.DMA((N_SEMS,)),
        pltpu.SemaphoreType.DMA((16,)),
    ]
    return pl.pallas_call(
        kernel,
        out_shape=(
            shape((TOK, D_OWN), BF16),
            shape((D_OWN, F_OWN), BF16),
            shape((D_OWN, F_OWN), BF16),
            shape((F_OWN, D_OWN), BF16),
        ),
        in_specs=[vmem] * 7,
        out_specs=(vmem,) * 4,
        scratch_shapes=scratch,
        compiler_params=pltpu.CompilerParams(
            collective_id=0, has_side_effects=True, vmem_limit_bytes=56 * 1024 * 1024
        ),
        cost_estimate=pl.CostEstimate(
            flops=3_700_000_000, bytes_accessed=3_000_000, transcendentals=400_000
        ),
    )(
        inputs,
        cotangent,
        gate_pre.reshape(2, TOK, F_OWN),
        up_pre.reshape(2, TOK, F_OWN),
        gate_weight,
        up_weight,
        down_weight,
    )


def solution(mesh):
    placed = (
        P("col", "row"),
        P("col", "row"),
        P("row", "col"),
        P("row", "col"),
        P("row", "col"),
        P("row", "col"),
        P("col", "row"),
    )
    return jax.shard_map(
        on_device,
        mesh=mesh,
        in_specs=placed,
        out_specs=(P("col", "row"), P("row", "col"), P("row", "col"), P("col", "row")),
        check_vma=False,
    )
```

```python
import jax
import jax.numpy as jnp
from jax import lax
from jax.experimental import pallas as pl
from jax.experimental.pallas import tpu as pltpu
from jax.sharding import PartitionSpec as P

MESH = pl.DeviceIdType.MESH
BF16 = jnp.bfloat16
F32 = jnp.float32

N_X, N_Y, N_Z = 4, 8, 8
TOK = 48
D_OWN = 384
D_CHIP = 768
F_OWN = 512
CHUNK = 192
F_PART = 128
N_SEMS = 200


def nt_dot(left, right):
    return lax.dot_general(left, right, (((1,), (1,)), ((), ())), preferred_element_type=F32)


def tn_dot(left, right):
    return lax.dot_general(left, right, (((0,), (0,)), ((), ())), preferred_element_type=F32)


def kernel(
    inp_in, cot_in, gate_in, up_in, wg_in, wu_in, wd_in,
    ig_out, gg_out, ug_out, dg_out,
    cot, inp, gate, up, wg, wu, wd,
    part, part16, near_got, far_got, half_got, pair_got, pair_send, hgrad,
    lin_g, lin_u, hidden, delta_g, delta_u,
    ig_mine, xs_send, xs_got, ys_send, ys_got,
    dg_send, gg_send, ug_send, dg_got, gg_got, ug_got, dg_own, gg_own, ug_own,
    ig_sum, gg_sum, ug_sum, dg_sum,
    send_sems, recv_sems, local_sems, cot_sems, inp_sems, ys_sems,
):
    row = lax.axis_index("row")
    col = lax.axis_index("col")
    z, core = row // 2, row % 2
    x, y = col // N_Y, col % N_Y

    def at_z(dz):
        return (((z + dz + N_Z) % N_Z) * 2 + core, col)

    def at_x(dx):
        return (row, ((x + dx + N_X) % N_X) * N_Y + y)

    def at_y(dy, on_core):
        return (z * 2 + on_core, x * N_Y + (y + dy) % N_Y)

    sib = at_y(0, 1 - core)

    copies = []
    local = []

    def send(src, dst, device):
        k = len(copies)
        cp = pltpu.make_async_remote_copy(
            src_ref=src, dst_ref=dst, send_sem=send_sems.at[k], recv_sem=recv_sems.at[k],
            device_id=device, device_id_type=MESH,
        )
        cp.start()
        copies.append(cp)
        return cp

    def move(src, dst):
        cp = pltpu.make_async_copy(src, dst, local_sems.at[len(local)])
        cp.start()
        local.append(cp)
        return cp

    barrier = pltpu.get_barrier_semaphore()
    others = [sib] + [at_y(dy, c) for dy in range(1, N_Y) for c in (0, 1)]
    others += [at_x(dx) for dx in (1, 2, 3)] + [at_z(dz) for dz in (1, 2, 6, 7)]
    for dev in others:
        pl.semaphore_signal(barrier, inc=1, device_id=dev, device_id_type=MESH)
    pl.semaphore_wait(barrier, len(others))

    lo, hi = pl.ds(0, D_OWN), pl.ds(D_OWN, D_OWN)

    def chunk_of(xx):
        dx = (xx - x + N_X) % N_X
        return dx + (dx // 2) * (5 - 2 * dx)

    c_y, k_y, h_y = (y // 2) % 2, y // 4, y % 2
    side = (core + c_y) % 2
    y_sem = (k_y * 2 + h_y) * 2 + side
    late_sends = []

    def over_y(src, buf, sems):
        dst = buf.at[0, k_y, h_y, :, pl.ds(pl.multiple_of(side * D_OWN, 128), D_OWN)]

        def copy(k, device):
            return pltpu.make_async_remote_copy(
                src_ref=src, dst_ref=dst, send_sem=send_sems.at[k], recv_sem=sems.at[y_sem],
                device_id=device, device_id_type=MESH,
            )

        for dy in (4, 3, 5, 2, 6, 1, 7):
            cp = copy(len(copies), at_y(dy, c_y))
            cp.start()
            copies.append(cp)
        k = N_SEMS - 1 - len(late_sends)
        late_sends.append((lambda: copy(k, sib), side == 1))

        @pl.when(side == 0)
        def _():
            pltpu.make_async_copy(src, dst, sems.at[y_sem]).start()

        @pl.when(side == 1)
        def _():
            copy(k, sib).start()

    def over_y_wait(buf, sems):
        for k in (0, 1):
            for h in (0, 1):
                for s, cols in ((0, lo), (1, hi)):
                    dst = buf.at[0, k, h, :, cols]
                    pltpu.make_async_copy(dst, dst, sems.at[(k * 2 + h) * 2 + s]).wait()

    def over_x(buf):
        return [send(buf.at[0], buf.at[r], at_x(dx)) for dx, r in ((2, 3), (1, 2), (3, 1))]

    class Ring:
        def __init__(self, buf, own, long_way):
            self.buf, self.own = buf, own
            self.hops = {long_way: N_Z // 2, -long_way: N_Z // 2 - 1}
            self.cps = {}

        def slot(self, zz):
            return self.buf.at[chunk_of(zz // 2), zz % 2]

        def start(self, s):
            for way in (+1, -1):
                if s <= self.hops[way]:
                    owner = (z - way * (s - 1) + N_Z) % N_Z
                    src = self.own if s == 1 else self.slot(owner)
                    self.cps[way, s] = send(src, self.slot(owner), at_z(way))

        def wait(self, s):
            for way in (+1, -1):
                if s <= self.hops[way]:
                    self.cps[way, s].wait_recv()

    def piece(buf, r, dz, rows=pl.ds(0, 2 * TOK)):
        o = (z + dz + N_Z) % N_Z
        return buf.at[r, o // 4, rows, pl.ds(pl.multiple_of((o % 4) * F_PART, F_PART), F_PART)]

    halves = {+1: pl.ds(0, TOK), -1: pl.ds(TOK, TOK)}

    class SumOverZ:
        def __init__(self, r):
            self.r = r
            self.cps = {}

        def first(self):
            r = self.r
            for i, way in enumerate((+1, -1)):
                self.cps["far", way] = send(piece(part16, r, 3 * way), far_got.at[r, i], at_z(way))
                self.cps["half", way] = send(
                    piece(part16, r, 4, halves[way]), half_got.at[r, i], at_z(2 * way)
                )
            for i, way in enumerate((+1, -1)):
                self.cps["near", way] = send(piece(part16, r, way), near_got.at[r, i], at_z(way))

        def second(self):
            r = self.r
            for i, way in enumerate((+1, -1)):
                self.cps["far", way].wait_recv()
                self.cps["half", way].wait_recv()
                total = piece(part, r, 2 * way)[...] + far_got[r, i].astype(F32)
                extra = half_got[r, i].astype(F32)
                rest = jnp.zeros_like(extra)
                rows = (extra, rest) if way == 1 else (rest, extra)
                pair_send[r, i] = (total + jnp.concatenate(rows, axis=0)).astype(BF16)
                self.cps["pair", way] = send(pair_send.at[r, i], pair_got.at[r, i], at_z(2 * way))

        def third(self):
            r = self.r
            total = piece(part, r, 0)[...]
            for i, way in enumerate((+1, -1)):
                self.cps["near", way].wait_recv()
                total = total + near_got[r, i].astype(F32)
            for i, way in enumerate((+1, -1)):
                self.cps["pair", way].wait_recv()
                total = total + pair_got[r, i].astype(F32)
            own = piece(hgrad, r, 0)
            own[...] = total.astype(BF16)
            for way in (+1, -1):
                self.cps["all2", way] = send(own, own, at_z(2 * way))
            for way in (+1, -1):
                self.cps["all1", way] = send(own, own, at_z(way))

        def fourth(self):
            r = self.r
            for way in (+1, -1):
                self.cps["all2", way].wait_recv()
                got = piece(hgrad, r, -2 * way)
                self.cps["all3", way] = send(got, got, at_z(way))
                got = piece(hgrad, r, -2 * way, halves[way])
                self.cps["all4", way] = send(got, got, at_z(2 * way))

        def last(self):
            for way in (+1, -1):
                for name in ("all1", "all3", "all4"):
                    self.cps[name, way].wait_recv()

    def partial_sums(r):
        left = cot[r].reshape(CHUNK, D_CHIP)
        for n in (0, 1):
            cols = pl.ds(n * 256, 256)
            value = nt_dot(left, wd[cols, :]).reshape(2, 2 * TOK, 256)
            part[r, :, :, cols] = value
            part16[r, :, :, cols] = value.astype(BF16)

    def activations(r):
        @pl.loop(0, 4)
        def _(i):
            rows = pl.ds(pl.multiple_of((i % 2) * TOK, TOK), TOK)
            g = gate[r, i // 2, rows].astype(F32)
            u = up[r, i // 2, rows].astype(F32)
            s = 1.0 / (1.0 + jnp.exp(-g))
            silu = g * s
            hidden[r, i // 2, rows] = (silu * u).astype(BF16)
            lin_g[r, i // 2, rows] = u * s * (1.0 + g * (1.0 - s))
            lin_u[r, i // 2, rows] = silu

    def deltas(r):
        @pl.loop(0, 4)
        def _(i):
            rows = pl.ds(pl.multiple_of((i % 2) * TOK, TOK), TOK)
            hg = hgrad[r, i // 2, rows].astype(F32)
            delta_g[r, i // 2, rows] = (hg * lin_g[r, i // 2, rows]).astype(BF16)
            delta_u[r, i // 2, rows] = (hg * lin_u[r, i // 2, rows]).astype(BF16)

    def input_part(r):
        left_g = delta_g[r].reshape(CHUNK, F_OWN)
        left_u = delta_u[r].reshape(CHUNK, F_OWN)
        for i in range(D_CHIP // 256):
            n = pl.ds(i * 256, 256)
            term = nt_dot(left_g, wg[n, :]) + nt_dot(left_u, wu[n, :])
            term = term.reshape(2, 2 * TOK, 256)
            if r == 0:
                ig_mine[:, :, n] = term
            else:
                xs_send[r - 1, :, :, n] = term.astype(BF16)

    xs_cps = {}

    def send_x(r):
        dx = {1: 1, 2: 3, 3: 2}[r]
        for k in (0, 1):
            xs_cps[r, k] = send(xs_send.at[r - 1, k], xs_got.at[r - 1, k], at_x(dx))

    late_ys = []

    def send_y(k):
        total = ig_mine[k]
        for r in (1, 2, 3):
            xs_cps[r, k].wait_recv()
            total = total + xs_got[r - 1, k].astype(F32)
        ys_send[k] = total.astype(BF16)
        for h in (0, 1):
            yy = 4 * k + 2 * core + h
            rows = pl.ds(h * TOK, TOK)

            def copy(q, cols, on_core, rows=rows, yy=yy):
                return pltpu.make_async_remote_copy(
                    src_ref=ys_send.at[k, rows, cols], dst_ref=ys_got.at[y],
                    send_sem=send_sems.at[q], recv_sem=ys_sems.at[y],
                    device_id=(z * 2 + on_core, x * N_Y + yy), device_id_type=MESH,
                )

            cp = copy(len(copies), hi, 1 - core)
            cp.start()
            copies.append(cp)
            q = N_SEMS - 1 - len(late_sends)
            late_sends.append((lambda q=q, copy=copy: copy(q, lo, core), yy != y))

            @pl.when(yy != y)
            def _(q=q, copy=copy):
                copy(q, lo, core).start()

            @pl.when(yy == y)
            def _(k=k, rows=rows):
                pltpu.make_async_copy(ys_send.at[k, rows, lo], ys_got.at[y], ys_sems.at[y]).start()

    def flat(buf, first, count, width):
        return buf.at[pl.ds(first, count)].reshape(count * CHUNK, width)

    def down_grad():
        left = flat(hidden, 0, 4, F_OWN)
        right = flat(cot, 0, 4, D_CHIP)

        @pl.loop(0, F_OWN // 128)
        def _(i):
            rows = pl.ds(pl.multiple_of(i * 128, 128), 128)
            both = tn_dot(left[:, rows], right[...])
            dg_own[rows, :] = both[:, :D_OWN]
            dg_send[rows, :] = both[:, D_OWN:].astype(BF16)

        return send(dg_send, dg_got, sib)

    def weight_grad(delta, own, first, count, sent=None):
        left = flat(inp, first, count, D_CHIP)
        right = flat(delta, first, count, F_OWN)

        @pl.loop(0, D_CHIP // 128)
        def _(i):
            rows = pl.ds(pl.multiple_of(i * 128, 128), 128)
            value = tn_dot(left[:, rows], right[...])
            if first > 0:
                value = value + own[rows, :]
            own[rows, :] = value

        if sent is not None:
            sent[...] = own[hi, :].astype(BF16)

    def finish(own, got, cp, total, out):
        cp.wait_recv()
        total[...] = (own[pl.ds(0, total.shape[0]), :] + got[...].astype(F32)).astype(BF16)
        return move(total, out)

    over_y(cot_in, cot, cot_sems)
    gate_ring = Ring(gate, gate_in, +1)
    up_ring = Ring(up, up_in, -1)
    gate_ring.start(1)
    up_ring.start(1)
    wd_self = move(wd_in, wd.at[:, lo])
    wd_cp = send(wd_in, wd.at[:, hi], sib)
    gate_self = move(gate_in, gate_ring.slot(z))
    up_self = move(up_in, up_ring.slot(z))

    over_y_wait(cot, cot_sems)
    cot_cps = over_x(cot)
    over_y(inp_in, inp, inp_sems)
    wd_self.wait()
    wd_cp.wait_recv()
    partial_sums(0)
    sums = [SumOverZ(r) for r in range(4)]
    sums[0].first()
    gate_ring.wait(1)
    gate_ring.start(2)
    up_ring.wait(1)
    up_ring.start(2)
    wg_self = move(wg_in, wg.at[lo])
    wu_self = move(wu_in, wu.at[lo])
    wg_cp = send(wg_in, wg.at[hi], sib)
    wu_cp = send(wu_in, wu.at[hi], sib)
    gate_self.wait()
    up_self.wait()

    sums[0].second()
    gate_ring.wait(2)
    gate_ring.start(3)
    up_ring.wait(2)
    up_ring.start(3)
    cot_cps[1].wait_recv()
    partial_sums(2)
    sums[2].first()
    cot_cps[2].wait_recv()
    partial_sums(1)
    sums[1].first()
    sums[0].third()
    cot_cps[0].wait_recv()
    partial_sums(3)
    sums[3].first()
    over_y_wait(inp, inp_sems)
    inp_cps = over_x(inp)
    gate_ring.wait(3)
    gate_ring.start(4)
    up_ring.wait(3)
    up_ring.start(4)
    sums[2].second()
    sums[1].second()
    sums[0].fourth()
    sums[3].second()
    sums[2].third()
    sums[1].third()
    gate_ring.wait(4)
    up_ring.wait(4)
    activations(0)
    sums[3].third()
    activations(2)
    activations(1)
    sums[2].fourth()
    sums[1].fourth()
    activations(3)
    wg_self.wait()
    wu_self.wait()
    wg_cp.wait_recv()
    wu_cp.wait_recv()
    sums[0].last()
    deltas(0)
    input_part(0)
    sums[3].fourth()
    sums[2].last()
    deltas(2)
    input_part(2)
    send_x(2)
    sums[1].last()
    deltas(1)
    input_part(1)
    send_x(1)
    dg_cp = down_grad()
    sums[3].last()
    deltas(3)
    input_part(3)
    send_x(3)
    for cp in inp_cps:
        cp.wait_recv()
    weight_grad(delta_g, gg_own, 0, 3)
    weight_grad(delta_g, gg_own, 3, 1, gg_send)
    gg_cp = send(gg_send, gg_got, sib)
    outs = [finish(dg_own, dg_got, dg_cp, dg_sum, dg_out)]
    send_y(0)
    send_y(1)
    weight_grad(delta_u, ug_own, 0, 3)
    weight_grad(delta_u, ug_own, 3, 1, ug_send)
    ug_cp = send(ug_send, ug_got, sib)
    outs.append(finish(gg_own, gg_got, gg_cp, gg_sum, gg_out))
    outs.append(finish(ug_own, ug_got, ug_cp, ug_sum, ug_out))

    total = jnp.zeros((TOK, D_OWN), F32)
    for yy in range(N_Y):
        dst = ys_got.at[yy]
        pltpu.make_async_copy(dst, dst, ys_sems.at[yy]).wait()
        total = total + ys_got[yy].astype(F32)
    ig_sum[...] = total.astype(BF16)
    outs.append(move(ig_sum, ig_out))

    for cp in copies:
        cp.wait_send()
    for make, remote in late_sends:
        @pl.when(remote)
        def _(make=make):
            make().wait_send()
    for cp in outs:
        cp.wait()


def copy_kernel(a, b, c, d, a_out, b_out, c_out, d_out, a_buf, b_buf, c_buf, d_buf, sems):
    sets = ((a, a_buf, a_out), (b, b_buf, b_out), (c, c_buf, c_out), (d, d_buf, d_out))
    reads = [pltpu.make_async_copy(src, buf, sems.at[i]) for i, (src, buf, _) in enumerate(sets)]
    writes = [pltpu.make_async_copy(buf, dst, sems.at[4 + i]) for i, (_, buf, dst) in enumerate(sets)]
    for cp in reads:
        cp.start()
    for before, cp in zip(reads, writes):
        before.wait()
        cp.start()
    for cp in writes:
        cp.wait()


def on_device(inputs, cotangent, gate_pre, up_pre, gate_weight, up_weight, down_weight):
    vmem = pl.BlockSpec(memory_space=pltpu.VMEM)
    hbm = pl.BlockSpec(memory_space=pl.ANY)
    shape = jax.ShapeDtypeStruct
    outs = (
        shape((TOK, D_OWN), BF16),
        shape((D_OWN, F_OWN), BF16),
        shape((D_OWN, F_OWN), BF16),
        shape((F_OWN, D_OWN), BF16),
    )
    by_token = lambda width, kind: pltpu.VMEM((4, 2, 2 * TOK, width), kind)
    z_piece = pltpu.VMEM((4, 2, 2 * TOK, F_PART), BF16)
    scratch = [
        pltpu.VMEM((4, 2, 2, TOK, D_CHIP), BF16),
        pltpu.VMEM((4, 2, 2, TOK, D_CHIP), BF16),
        by_token(F_OWN, BF16),
        by_token(F_OWN, BF16),
        pltpu.VMEM((D_CHIP, F_OWN), BF16),
        pltpu.VMEM((D_CHIP, F_OWN), BF16),
        pltpu.VMEM((F_OWN, D_CHIP), BF16),
        by_token(F_OWN, F32),
        by_token(F_OWN, BF16),
        z_piece,
        z_piece,
        pltpu.VMEM((4, 2, TOK, F_PART), BF16),
        z_piece,
        z_piece,
        by_token(F_OWN, BF16),
        by_token(F_OWN, F32),
        by_token(F_OWN, F32),
        by_token(F_OWN, BF16),
        by_token(F_OWN, BF16),
        by_token(F_OWN, BF16),
        pltpu.VMEM((2, 2 * TOK, D_CHIP), F32),
        pltpu.VMEM((3, 2, 2 * TOK, D_CHIP), BF16),
        pltpu.VMEM((3, 2, 2 * TOK, D_CHIP), BF16),
        pltpu.VMEM((2, 2 * TOK, D_CHIP), BF16),
        pltpu.VMEM((N_Y, TOK, D_OWN), BF16),
        pltpu.VMEM((F_OWN, D_OWN), BF16),
        pltpu.VMEM((D_OWN, F_OWN), BF16),
        pltpu.VMEM((D_OWN, F_OWN), BF16),
        pltpu.VMEM((F_OWN, D_OWN), BF16),
        pltpu.VMEM((D_OWN, F_OWN), BF16),
        pltpu.VMEM((D_OWN, F_OWN), BF16),
        pltpu.VMEM((F_OWN, D_OWN), F32),
        pltpu.VMEM((D_CHIP, F_OWN), F32),
        pltpu.VMEM((D_CHIP, F_OWN), F32),
        pltpu.VMEM((TOK, D_OWN), BF16),
        pltpu.VMEM((D_OWN, F_OWN), BF16),
        pltpu.VMEM((D_OWN, F_OWN), BF16),
        pltpu.VMEM((F_OWN, D_OWN), BF16),
        pltpu.SemaphoreType.DMA((N_SEMS,)),
        pltpu.SemaphoreType.DMA((N_SEMS,)),
        pltpu.SemaphoreType.DMA((16,)),
        pltpu.SemaphoreType.DMA((8,)),
        pltpu.SemaphoreType.DMA((8,)),
        pltpu.SemaphoreType.DMA((8,)),
    ]
    grads = pl.pallas_call(
        kernel,
        out_shape=outs,
        in_specs=[vmem, vmem] + [hbm] * 5,
        out_specs=(hbm,) * 4,
        scratch_shapes=scratch,
        compiler_params=pltpu.CompilerParams(
            collective_id=0, has_side_effects=True, vmem_limit_bytes=56 * 1024 * 1024
        ),
        cost_estimate=pl.CostEstimate(
            flops=3_700_000_000, bytes_accessed=3_000_000, transcendentals=400_000
        ),
    )(inputs, cotangent, gate_pre, up_pre, gate_weight, up_weight, down_weight)
    return pl.pallas_call(
        copy_kernel,
        out_shape=outs,
        in_specs=[hbm] * 4,
        out_specs=(hbm,) * 4,
        scratch_shapes=[pltpu.VMEM(out.shape, out.dtype) for out in outs]
        + [pltpu.SemaphoreType.DMA((8,))],
    )(*grads)


def solution(mesh):
    placed = (
        P("col", "row"),
        P("col", "row"),
        P("row", "col"),
        P("row", "col"),
        P("row", "col"),
        P("row", "col"),
        P("col", "row"),
    )
    return jax.shard_map(
        on_device,
        mesh=mesh,
        in_specs=placed,
        out_specs=(P("col", "row"), P("row", "col"), P("row", "col"), P("col", "row")),
        check_vma=False,
    )
```

```python
import jax
import jax.numpy as jnp
from jax import lax
from jax.experimental import pallas as pl
from jax.experimental.pallas import tpu as pltpu
from jax.sharding import PartitionSpec as P

MESH = pl.DeviceIdType.MESH
BF16 = jnp.bfloat16
F32 = jnp.float32

N_X, N_Y, N_Z = 4, 8, 8
TOK = 48
D_OWN = 384
D_CHIP = 768
F_OWN = 512
CHUNK = 192
F_PART = 128
N_SEMS = 220


def nt_dot(left, right):
    return lax.dot_general(left, right, (((1,), (1,)), ((), ())), preferred_element_type=F32)


def tn_dot(left, right):
    return lax.dot_general(left, right, (((0,), (0,)), ((), ())), preferred_element_type=F32)


def kernel(
    inp_in, cot_in, gate_in, up_in, wg_in, wu_in, wd_in,
    ig_out, gg_out, ug_out, dg_out,
    cot, inp, gate, up, wg, wu, wd,
    part, part16, near_got, far_got, half_got, pair_got, pair_send, hgrad,
    lin_g, lin_u, hidden, delta_g, delta_u,
    ig_mine, xs_send, xs_got, ys_send, ys_got,
    dg_send, gg_send, ug_send, dg_got, gg_got, ug_got, dg_own, gg_own, ug_own,
    ig_sum, gg_sum, ug_sum, dg_sum,
    cot_far, inp_far, yf_got, far_sum, far_back,
    send_sems, recv_sems, local_sems, cot_sems, inp_sems, ys_sems,
    cot_far_sems, inp_far_sems, yf_sems,
):
    row = lax.axis_index("row")
    col = lax.axis_index("col")
    z, core = row // 2, row % 2
    x, y = col // N_Y, col % N_Y

    def at_z(dz):
        return (((z + dz + N_Z) % N_Z) * 2 + core, col)

    def at_x(dx):
        return (row, ((x + dx + N_X) % N_X) * N_Y + y)

    def at_y(dy, on_core):
        return (z * 2 + on_core, x * N_Y + (y + dy) % N_Y)

    sib = at_y(0, 1 - core)

    copies = []
    local = []

    def send(src, dst, device):
        k = len(copies)
        cp = pltpu.make_async_remote_copy(
            src_ref=src, dst_ref=dst, send_sem=send_sems.at[k], recv_sem=recv_sems.at[k],
            device_id=device, device_id_type=MESH,
        )
        cp.start()
        copies.append(cp)
        return cp

    def move(src, dst):
        cp = pltpu.make_async_copy(src, dst, local_sems.at[len(local)])
        cp.start()
        local.append(cp)
        return cp

    lo, hi = pl.ds(0, D_OWN), pl.ds(D_OWN, D_OWN)

    wd_self = move(wd_in, wd.at[:, lo])
    wg_self = move(wg_in, wg.at[lo])
    wu_self = move(wu_in, wu.at[lo])

    barrier = pltpu.get_barrier_semaphore()
    others = [sib] + [at_y(dy, c) for dy in range(1, N_Y) for c in (0, 1)]
    others += [at_x(dx) for dx in (1, 2, 3)] + [at_z(dz) for dz in (1, 2, 6, 7)]
    for dev in others:
        pl.semaphore_signal(barrier, inc=1, device_id=dev, device_id_type=MESH)
    pl.semaphore_wait(barrier, len(others))

    def chunk_of(xx):
        dx = (xx - x + N_X) % N_X
        return dx + (dx // 2) * (5 - 2 * dx)

    c_y, k_y, h_y = (y // 2) % 2, y // 4, y % 2
    side = (core + c_y) % 2
    y_sem = (k_y * 2 + h_y) * 2 + side
    late_sends = []

    def over_y(src, buf, r, sems):
        dst = buf.at[r, k_y, h_y, :, pl.ds(pl.multiple_of(side * D_OWN, 128), D_OWN)]

        def copy(k, device):
            return pltpu.make_async_remote_copy(
                src_ref=src, dst_ref=dst, send_sem=send_sems.at[k], recv_sem=sems.at[y_sem],
                device_id=device, device_id_type=MESH,
            )

        for dy in (1, 7, 2, 6, 3, 5, 4):
            cp = copy(len(copies), at_y(dy, c_y))
            cp.start()
            copies.append(cp)
        k = N_SEMS - 1 - len(late_sends)
        late_sends.append((lambda: copy(k, sib), side == 1))

        @pl.when(side == 0)
        def _():
            pltpu.make_async_copy(src, dst, sems.at[y_sem]).start()

        @pl.when(side == 1)
        def _():
            copy(k, sib).start()

    def over_y_wait(buf, r, sems, k):
        for h in (0, 1):
            for s, cols in ((0, lo), (1, hi)):
                dst = buf.at[r, k, h, :, cols]
                pltpu.make_async_copy(dst, dst, sems.at[(k * 2 + h) * 2 + s]).wait()

    k_near = (((y - 2 * core + N_Y) % N_Y + 1) // 4) % 2

    def over_x(buf, k):
        return {
            r: send(buf.at[0, k], buf.at[r, k], at_x(dx)) for dx, r in ((1, 2), (3, 1))
        }

    def over_x_wait(parts, r):
        for cps in parts:
            cps[r].wait_recv()

    class Ring:
        def __init__(self, buf, own, long_way, h):
            self.rows = pl.ds(h * TOK, TOK)
            self.buf, self.own = buf, own.at[self.rows]
            self.hops = {long_way: N_Z // 2, -long_way: N_Z // 2 - 1}
            self.cps = {}

        def slot(self, zz):
            return self.buf.at[chunk_of(zz // 2), zz % 2, self.rows]

        def start(self, s):
            for way in (+1, -1):
                if s <= self.hops[way]:
                    owner = (z - way * (s - 1) + N_Z) % N_Z
                    src = self.own if s == 1 else self.slot(owner)
                    self.cps[way, s] = send(src, self.slot(owner), at_z(way))

        def wait(self, s):
            for way in (+1, -1):
                if s <= self.hops[way]:
                    self.cps[way, s].wait_recv()

        def step(self, s):
            self.wait(s)
            self.start(s + 1)

    def piece(buf, r, dz, rows=pl.ds(0, 2 * TOK)):
        o = (z + dz + N_Z) % N_Z
        return buf.at[r, o // 4, rows, pl.ds(pl.multiple_of((o % 4) * F_PART, F_PART), F_PART)]

    halves = {+1: pl.ds(0, TOK), -1: pl.ds(TOK, TOK)}

    class SumOverZ:
        def __init__(self, r):
            self.r = r
            self.cps = {}

        def first(self):
            r = self.r
            for i, way in enumerate((+1, -1)):
                self.cps["far", way] = send(piece(part16, r, 3 * way), far_got.at[r, i], at_z(way))
                self.cps["half", way] = send(
                    piece(part16, r, 4, halves[way]), half_got.at[r, i], at_z(2 * way)
                )
            for i, way in enumerate((+1, -1)):
                self.cps["near", way] = send(piece(part16, r, way), near_got.at[r, i], at_z(way))

        def second(self):
            r = self.r
            for i, way in enumerate((+1, -1)):
                self.cps["far", way].wait_recv()
                self.cps["half", way].wait_recv()
                total = piece(part, r, 2 * way)[...] + far_got[r, i].astype(F32)
                extra = half_got[r, i].astype(F32)
                rest = jnp.zeros_like(extra)
                rows = (extra, rest) if way == 1 else (rest, extra)
                pair_send[r, i] = (total + jnp.concatenate(rows, axis=0)).astype(BF16)
                self.cps["pair", way] = send(pair_send.at[r, i], pair_got.at[r, i], at_z(2 * way))

        def third(self):
            r = self.r
            total = piece(part, r, 0)[...]
            for i, way in enumerate((+1, -1)):
                self.cps["near", way].wait_recv()
                total = total + near_got[r, i].astype(F32)
            for i, way in enumerate((+1, -1)):
                self.cps["pair", way].wait_recv()
                total = total + pair_got[r, i].astype(F32)
            own = piece(hgrad, r, 0)
            own[...] = total.astype(BF16)
            for way in (+1, -1):
                self.cps["all2", way] = send(own, own, at_z(2 * way))
            for way in (+1, -1):
                self.cps["all1", way] = send(own, own, at_z(way))

        def fourth(self):
            r = self.r
            for way in (+1, -1):
                self.cps["all2", way].wait_recv()
                got = piece(hgrad, r, -2 * way)
                self.cps["all3", way] = send(got, got, at_z(way))
                got = piece(hgrad, r, -2 * way, halves[way])
                self.cps["all4", way] = send(got, got, at_z(2 * way))

        def last(self):
            for way in (+1, -1):
                for name in ("all1", "all3", "all4"):
                    self.cps[name, way].wait_recv()

    def partial_sums(r):
        left = cot[r].reshape(CHUNK, D_CHIP)
        for n in (0, 1):
            cols = pl.ds(n * 256, 256)
            value = nt_dot(left, wd[cols, :]).reshape(2, 2 * TOK, 256)
            part[r, :, :, cols] = value
            part16[r, :, :, cols] = value.astype(BF16)

    def activations(r):
        @pl.loop(0, 4)
        def _(i):
            rows = pl.ds(pl.multiple_of((i % 2) * TOK, TOK), TOK)
            g = gate[r, i // 2, rows].astype(F32)
            u = up[r, i // 2, rows].astype(F32)
            s = 1.0 / (1.0 + jnp.exp(-g))
            silu = g * s
            hidden[r, i // 2, rows] = (silu * u).astype(BF16)
            lin_g[r, i // 2, rows] = u * s * (1.0 + g * (1.0 - s))
            lin_u[r, i // 2, rows] = silu

    def deltas(r):
        @pl.loop(0, 4)
        def _(i):
            rows = pl.ds(pl.multiple_of((i % 2) * TOK, TOK), TOK)
            hg = hgrad[r, i // 2, rows].astype(F32)
            delta_g[r, i // 2, rows] = (hg * lin_g[r, i // 2, rows]).astype(BF16)
            delta_u[r, i // 2, rows] = (hg * lin_u[r, i // 2, rows]).astype(BF16)

    def input_part(r):
        left_g = delta_g[r].reshape(CHUNK, F_OWN)
        left_u = delta_u[r].reshape(CHUNK, F_OWN)
        for i in range(D_CHIP // 256):
            n = pl.ds(i * 256, 256)
            term = nt_dot(left_g, wg[n, :]) + nt_dot(left_u, wu[n, :])
            term = term.reshape(2, 2 * TOK, 256)
            if r == 0:
                ig_mine[:, :, n] = term
            else:
                xs_send[r - 1, :, :, n] = term.astype(BF16)

    xs_cps = {}

    def send_x(r):
        dx = {1: 1, 2: 3}[r]
        for k in (0, 1):
            xs_cps[r, k] = send(xs_send.at[r - 1, k], xs_got.at[r - 1, k], at_x(dx))

    def sum_x(k):
        total = ig_mine[k]
        for r in (1, 2):
            xs_cps[r, k].wait_recv()
            total = total + xs_got[r - 1, k].astype(F32)
        ys_send[k] = total.astype(BF16)

    def send_y(src, k, got, sems):
        for h in (0, 1):
            yy = 4 * k + 2 * core + h
            rows = pl.ds(h * TOK, TOK)

            def copy(q, cols, on_core, rows=rows, yy=yy):
                return pltpu.make_async_remote_copy(
                    src_ref=src.at[k, rows, cols], dst_ref=got.at[y],
                    send_sem=send_sems.at[q], recv_sem=sems.at[y],
                    device_id=(z * 2 + on_core, x * N_Y + yy), device_id_type=MESH,
                )

            cp = copy(len(copies), hi, 1 - core)
            cp.start()
            copies.append(cp)
            q = N_SEMS - 1 - len(late_sends)
            late_sends.append((lambda q=q, copy=copy: copy(q, lo, core), yy != y))

            @pl.when(yy != y)
            def _(q=q, copy=copy):
                copy(q, lo, core).start()

            @pl.when(yy == y)
            def _(rows=rows):
                pltpu.make_async_copy(src.at[k, rows, lo], got.at[y], sems.at[y]).start()

    def sum_y(got, sems):
        total = jnp.zeros((TOK, D_OWN), F32)
        for yy in range(N_Y):
            dst = got.at[yy]
            pltpu.make_async_copy(dst, dst, sems.at[yy]).wait()
            total = total + got[yy].astype(F32)
        return total

    def flat(buf, first, count, width):
        return buf.at[pl.ds(first, count)].reshape(count * CHUNK, width)

    def down_grad():
        left = flat(hidden, 0, 4, F_OWN)
        right = flat(cot, 0, 4, D_CHIP)

        @pl.loop(0, F_OWN // 128)
        def _(i):
            rows = pl.ds(pl.multiple_of(i * 128, 128), 128)
            both = tn_dot(left[:, rows], right[...])
            dg_own[rows, :] = both[:, :D_OWN]
            dg_send[rows, :] = both[:, D_OWN:].astype(BF16)

        return send(dg_send, dg_got, sib)

    def weight_grad(delta, own, first, count, sent=None):
        left = flat(inp, first, count, D_CHIP)
        right = flat(delta, first, count, F_OWN)

        @pl.loop(0, D_CHIP // 128)
        def _(i):
            rows = pl.ds(pl.multiple_of(i * 128, 128), 128)
            value = tn_dot(left[:, rows], right[...])
            if first > 0:
                value = value + own[rows, :]
            own[rows, :] = value

        if sent is not None:
            sent[...] = own[hi, :].astype(BF16)

    def finish(own, got, cp, total, out):
        cp.wait_recv()
        total[...] = (own[pl.ds(0, total.shape[0]), :] + got[...].astype(F32)).astype(BF16)
        return move(total, out)

    cot_far_cp = send(cot_in, cot_far, at_x(2))
    over_y(cot_in, cot, 0, cot_sems)
    rings = [
        Ring(gate, gate_in, +1, 0), Ring(up, up_in, -1, 0),
        Ring(gate, gate_in, -1, 1), Ring(up, up_in, +1, 1),
    ]
    for ring in rings:
        ring.start(1)
    wd_self.wait()
    wd_cp = send(wd.at[:, lo], wd.at[:, hi], sib)
    gate_self = move(gate_in, gate.at[chunk_of(z // 2), z % 2])
    up_self = move(up_in, up.at[chunk_of(z // 2), z % 2])

    sums = [SumOverZ(r) for r in range(4)]
    rings[0].step(1)
    rings[1].step(1)
    over_y_wait(cot, 0, cot_sems, k_near)
    cot_far_cp.wait_recv()
    over_y(cot_far, cot, 3, cot_far_sems)
    cot_cps = [over_x(cot, k_near)]
    rings[2].step(1)
    rings[3].step(1)
    rings[0].step(2)
    over_y_wait(cot, 0, cot_sems, 1 - k_near)
    cot_cps.append(over_x(cot, 1 - k_near))
    rings[1].step(2)
    inp_far_cp = send(inp_in, inp_far, at_x(2))
    rings[2].step(2)
    wd_cp.wait_recv()
    partial_sums(0)
    sums[0].first()
    rings[3].step(2)
    wg_self.wait()
    wg_cp = send(wg.at[lo], wg.at[hi], sib)
    wu_self.wait()
    wu_cp = send(wu.at[lo], wu.at[hi], sib)
    rings[0].step(3)
    rings[1].step(3)
    rings[2].step(3)
    sums[0].second()
    rings[3].step(3)
    for r in (2, 1):
        over_x_wait(cot_cps, r)
        partial_sums(r)
        sums[r].first()
    for k in (0, 1):
        over_y_wait(cot, 3, cot_far_sems, k)
    partial_sums(3)
    sums[3].first()
    over_y(inp_in, inp, 0, inp_sems)
    inp_far_cp.wait_recv()
    over_y(inp_far, inp, 3, inp_far_sems)
    sums[0].third()
    sums[2].second()
    sums[1].second()
    sums[3].second()
    inp_cps = []
    for k in (0, 1):
        over_y_wait(inp, 0, inp_sems, k)
        inp_cps.append(over_x(inp, k))
    sums[0].fourth()
    sums[2].third()
    sums[1].third()
    sums[3].third()
    for ring in rings:
        ring.wait(4)
    gate_self.wait()
    up_self.wait()
    activations(0)
    activations(2)
    wg_cp.wait_recv()
    wu_cp.wait_recv()
    sums[2].fourth()
    sums[1].fourth()
    sums[3].fourth()
    activations(1)
    activations(3)
    sums[0].last()
    deltas(0)
    input_part(0)
    for r in (2, 1):
        sums[r].last()
        deltas(r)
        input_part(r)
        send_x(r)
    sums[3].last()
    deltas(3)
    input_part(3)
    for k in (0, 1):
        send_y(xs_send.at[2], k, yf_got, yf_sems)
    dg_cp = down_grad()
    for k in (0, 1):
        sum_x(k)
        send_y(ys_send, k, ys_got, ys_sems)
    for k in (0, 1):
        over_y_wait(inp, 3, inp_far_sems, k)
    for r in (1, 2):
        over_x_wait(inp_cps, r)
    weight_grad(delta_g, gg_own, 0, 4, gg_send)
    gg_cp = send(gg_send, gg_got, sib)
    far_sum[...] = sum_y(yf_got, yf_sems).astype(BF16)
    far_cp = send(far_sum, far_back, at_x(2))
    weight_grad(delta_u, ug_own, 0, 4, ug_send)
    ug_cp = send(ug_send, ug_got, sib)
    outs = [finish(dg_own, dg_got, dg_cp, dg_sum, dg_out)]
    outs.append(finish(gg_own, gg_got, gg_cp, gg_sum, gg_out))
    outs.append(finish(ug_own, ug_got, ug_cp, ug_sum, ug_out))
    for cp in copies:
        cp.wait_send()
    for make, remote in late_sends:
        @pl.when(remote)
        def _(make=make):
            make().wait_send()

    total = sum_y(ys_got, ys_sems)
    far_cp.wait_recv()
    ig_sum[...] = (total + far_back[...].astype(F32)).astype(BF16)
    outs.append(move(ig_sum, ig_out))
    for cp in outs:
        cp.wait()


def copy_kernel(a, b, c, d, a_out, b_out, c_out, d_out, a_buf, b_buf, c_buf, d_buf, sems):
    sets = ((a, a_buf, a_out), (b, b_buf, b_out), (c, c_buf, c_out), (d, d_buf, d_out))
    reads = [pltpu.make_async_copy(src, buf, sems.at[i]) for i, (src, buf, _) in enumerate(sets)]
    writes = [pltpu.make_async_copy(buf, dst, sems.at[4 + i]) for i, (_, buf, dst) in enumerate(sets)]
    for cp in reads:
        cp.start()
    for before, cp in zip(reads, writes):
        before.wait()
        cp.start()
    for cp in writes:
        cp.wait()


def on_device(inputs, cotangent, gate_pre, up_pre, gate_weight, up_weight, down_weight):
    vmem = pl.BlockSpec(memory_space=pltpu.VMEM)
    hbm = pl.BlockSpec(memory_space=pl.ANY)
    shape = jax.ShapeDtypeStruct
    outs = (
        shape((TOK, D_OWN), BF16),
        shape((D_OWN, F_OWN), BF16),
        shape((D_OWN, F_OWN), BF16),
        shape((F_OWN, D_OWN), BF16),
    )
    by_token = lambda width, kind: pltpu.VMEM((4, 2, 2 * TOK, width), kind)
    z_piece = pltpu.VMEM((4, 2, 2 * TOK, F_PART), BF16)
    scratch = [
        pltpu.VMEM((4, 2, 2, TOK, D_CHIP), BF16),
        pltpu.VMEM((4, 2, 2, TOK, D_CHIP), BF16),
        by_token(F_OWN, BF16),
        by_token(F_OWN, BF16),
        pltpu.VMEM((D_CHIP, F_OWN), BF16),
        pltpu.VMEM((D_CHIP, F_OWN), BF16),
        pltpu.VMEM((F_OWN, D_CHIP), BF16),
        by_token(F_OWN, F32),
        by_token(F_OWN, BF16),
        z_piece,
        z_piece,
        pltpu.VMEM((4, 2, TOK, F_PART), BF16),
        z_piece,
        z_piece,
        by_token(F_OWN, BF16),
        by_token(F_OWN, F32),
        by_token(F_OWN, F32),
        by_token(F_OWN, BF16),
        by_token(F_OWN, BF16),
        by_token(F_OWN, BF16),
        pltpu.VMEM((2, 2 * TOK, D_CHIP), F32),
        pltpu.VMEM((3, 2, 2 * TOK, D_CHIP), BF16),
        pltpu.VMEM((2, 2, 2 * TOK, D_CHIP), BF16),
        pltpu.VMEM((2, 2 * TOK, D_CHIP), BF16),
        pltpu.VMEM((N_Y, TOK, D_OWN), BF16),
        pltpu.VMEM((F_OWN, D_OWN), BF16),
        pltpu.VMEM((D_OWN, F_OWN), BF16),
        pltpu.VMEM((D_OWN, F_OWN), BF16),
        pltpu.VMEM((F_OWN, D_OWN), BF16),
        pltpu.VMEM((D_OWN, F_OWN), BF16),
        pltpu.VMEM((D_OWN, F_OWN), BF16),
        pltpu.VMEM((F_OWN, D_OWN), F32),
        pltpu.VMEM((D_CHIP, F_OWN), F32),
        pltpu.VMEM((D_CHIP, F_OWN), F32),
        pltpu.VMEM((TOK, D_OWN), BF16),
        pltpu.VMEM((D_OWN, F_OWN), BF16),
        pltpu.VMEM((D_OWN, F_OWN), BF16),
        pltpu.VMEM((F_OWN, D_OWN), BF16),
        pltpu.VMEM((TOK, D_OWN), BF16),
        pltpu.VMEM((TOK, D_OWN), BF16),
        pltpu.VMEM((N_Y, TOK, D_OWN), BF16),
        pltpu.VMEM((TOK, D_OWN), BF16),
        pltpu.VMEM((TOK, D_OWN), BF16),
        pltpu.SemaphoreType.DMA((N_SEMS,)),
        pltpu.SemaphoreType.DMA((N_SEMS,)),
        pltpu.SemaphoreType.DMA((16,)),
    ] + [pltpu.SemaphoreType.DMA((8,))] * 6
    grads = pl.pallas_call(
        kernel,
        out_shape=outs,
        in_specs=[vmem] * 4 + [hbm] * 3,
        out_specs=(hbm,) * 4,
        scratch_shapes=scratch,
        compiler_params=pltpu.CompilerParams(
            collective_id=0, has_side_effects=True, vmem_limit_bytes=56 * 1024 * 1024
        ),
        cost_estimate=pl.CostEstimate(
            flops=3_700_000_000, bytes_accessed=3_000_000, transcendentals=400_000
        ),
    )(inputs, cotangent, gate_pre, up_pre, gate_weight, up_weight, down_weight)
    return pl.pallas_call(
        copy_kernel,
        out_shape=outs,
        in_specs=[hbm] * 4,
        out_specs=(hbm,) * 4,
        scratch_shapes=[pltpu.VMEM(out.shape, out.dtype) for out in outs]
        + [pltpu.SemaphoreType.DMA((8,))],
    )(*grads)


def solution(mesh):
    placed = (
        P("col", "row"),
        P("col", "row"),
        P("row", "col"),
        P("row", "col"),
        P("row", "col"),
        P("row", "col"),
        P("col", "row"),
    )
    return jax.shard_map(
        on_device,
        mesh=mesh,
        in_specs=placed,
        out_specs=(P("col", "row"), P("row", "col"), P("row", "col"), P("col", "row")),
        check_vma=False,
    )
```

```python
import jax
import jax.numpy as jnp
from jax import lax
from jax.experimental import pallas as pl
from jax.experimental.pallas import tpu as pltpu
from jax.sharding import PartitionSpec as P

MESH = pl.DeviceIdType.MESH
BF16 = jnp.bfloat16
F32 = jnp.float32

N_X, N_Y, N_Z = 4, 8, 8
TOK = 48
D_OWN = 384
D_CHIP = 768
F_OWN = 512
CHUNK = 192
F_PART = 128
N_SEMS = 220


def nt_dot(left, right):
    return lax.dot_general(left, right, (((1,), (1,)), ((), ())), preferred_element_type=F32)


def tn_dot(left, right):
    return lax.dot_general(left, right, (((0,), (0,)), ((), ())), preferred_element_type=F32)


def kernel(
    inp_in, cot_in, gate_in, up_in, wg_in, wu_in, wd_in,
    ig_out, gg_out, ug_out, dg_out,
    cot, inp, gate, up, wg, wu, wd,
    part, part16, near_got, far_got, half_got, pair_got, pair_send, hgrad,
    lin_g, lin_u, hidden, delta_g, delta_u,
    ig_mine, xs_send, xs_got, ys_send, ys_got,
    dg_send, gg_send, ug_send, dg_got, gg_got, ug_got, dg_own, gg_own, ug_own,
    cot_far, inp_far, yf_got, far_sum, far_back,
    send_sems, recv_sems, local_sems, cot_sems, inp_sems, ys_sems,
    cot_far_sems, inp_far_sems, yf_sems,
):
    row = lax.axis_index("row")
    col = lax.axis_index("col")
    z, core = row // 2, row % 2
    x, y = col // N_Y, col % N_Y

    def at_z(dz):
        return (((z + dz + N_Z) % N_Z) * 2 + core, col)

    def at_x(dx):
        return (row, ((x + dx + N_X) % N_X) * N_Y + y)

    def at_y(dy, on_core):
        return (z * 2 + on_core, x * N_Y + (y + dy) % N_Y)

    sib = at_y(0, 1 - core)

    copies = []
    local = []

    def send(src, dst, device):
        k = len(copies)
        cp = pltpu.make_async_remote_copy(
            src_ref=src, dst_ref=dst, send_sem=send_sems.at[k], recv_sem=recv_sems.at[k],
            device_id=device, device_id_type=MESH,
        )
        cp.start()
        copies.append(cp)
        return cp

    def move(src, dst):
        cp = pltpu.make_async_copy(src, dst, local_sems.at[len(local)])
        cp.start()
        local.append(cp)
        return cp

    lo, hi = pl.ds(0, D_OWN), pl.ds(D_OWN, D_OWN)

    wd_self = move(wd_in, wd.at[:, lo])
    wg_self = move(wg_in, wg.at[lo])
    wu_self = move(wu_in, wu.at[lo])

    barrier = pltpu.get_barrier_semaphore()
    others = [sib] + [at_y(dy, c) for dy in range(1, N_Y) for c in (0, 1)]
    others += [at_x(dx) for dx in (1, 2, 3)] + [at_z(dz) for dz in (1, 2, 6, 7)]
    for dev in others:
        pl.semaphore_signal(barrier, inc=1, device_id=dev, device_id_type=MESH)
    pl.semaphore_wait(barrier, len(others))

    def chunk_of(xx):
        dx = (xx - x + N_X) % N_X
        return dx + (dx // 2) * (5 - 2 * dx)

    c_y, k_y, h_y = (y // 2) % 2, y // 4, y % 2
    side = (core + c_y) % 2
    y_sem = (k_y * 2 + h_y) * 2 + side
    late_sends = []

    def over_y(src, buf, r, sems):
        dst = buf.at[r, k_y, h_y, :, pl.ds(pl.multiple_of(side * D_OWN, 128), D_OWN)]

        def copy(k, device):
            return pltpu.make_async_remote_copy(
                src_ref=src, dst_ref=dst, send_sem=send_sems.at[k], recv_sem=sems.at[y_sem],
                device_id=device, device_id_type=MESH,
            )

        for dy in (1, 7, 2, 6, 3, 5, 4):
            cp = copy(len(copies), at_y(dy, c_y))
            cp.start()
            copies.append(cp)
        k = N_SEMS - 1 - len(late_sends)
        late_sends.append((lambda: copy(k, sib), side == 1))

        @pl.when(side == 0)
        def _():
            pltpu.make_async_copy(src, dst, sems.at[y_sem]).start()

        @pl.when(side == 1)
        def _():
            copy(k, sib).start()

    def over_y_wait(buf, r, sems, k):
        for h in (0, 1):
            for s, cols in ((0, lo), (1, hi)):
                dst = buf.at[r, k, h, :, cols]
                pltpu.make_async_copy(dst, dst, sems.at[(k * 2 + h) * 2 + s]).wait()

    k_near = (((y - 2 * core + N_Y) % N_Y + 1) // 4) % 2

    def over_x(buf, k):
        return {
            r: send(buf.at[0, k], buf.at[r, k], at_x(dx)) for dx, r in ((1, 2), (3, 1))
        }

    def over_x_wait(parts, r):
        for cps in parts:
            cps[r].wait_recv()

    class Ring:
        def __init__(self, buf, own, long_way, h):
            self.rows = pl.ds(h * TOK, TOK)
            self.buf, self.own = buf, own.at[self.rows]
            self.hops = {long_way: N_Z // 2, -long_way: N_Z // 2 - 1}
            self.cps = {}

        def slot(self, zz):
            return self.buf.at[chunk_of(zz // 2), zz % 2, self.rows]

        def start(self, s):
            for way in (+1, -1):
                if s <= self.hops[way]:
                    owner = (z - way * (s - 1) + N_Z) % N_Z
                    src = self.own if s == 1 else self.slot(owner)
                    self.cps[way, s] = send(src, self.slot(owner), at_z(way))

        def wait(self, s):
            for way in (+1, -1):
                if s <= self.hops[way]:
                    self.cps[way, s].wait_recv()

        def step(self, s):
            self.wait(s)
            self.start(s + 1)

    def piece(buf, r, dz, rows=pl.ds(0, 2 * TOK)):
        o = (z + dz + N_Z) % N_Z
        return buf.at[r, o // 4, rows, pl.ds(pl.multiple_of((o % 4) * F_PART, F_PART), F_PART)]

    halves = {+1: pl.ds(0, TOK), -1: pl.ds(TOK, TOK)}

    class SumOverZ:
        def __init__(self, r):
            self.r = r
            self.cps = {}

        def first(self):
            r = self.r
            for i, way in enumerate((+1, -1)):
                self.cps["far", way] = send(piece(part16, r, 3 * way), far_got.at[r, i], at_z(way))
                self.cps["half", way] = send(
                    piece(part16, r, 4, halves[way]), half_got.at[r, i], at_z(2 * way)
                )
            for i, way in enumerate((+1, -1)):
                self.cps["near", way] = send(piece(part16, r, way), near_got.at[r, i], at_z(way))

        def second(self):
            r = self.r
            for i, way in enumerate((+1, -1)):
                self.cps["far", way].wait_recv()
                self.cps["half", way].wait_recv()
                total = piece(part, r, 2 * way)[...] + far_got[r, i].astype(F32)
                extra = half_got[r, i].astype(F32)
                rest = jnp.zeros_like(extra)
                rows = (extra, rest) if way == 1 else (rest, extra)
                pair_send[r, i] = (total + jnp.concatenate(rows, axis=0)).astype(BF16)
                self.cps["pair", way] = send(pair_send.at[r, i], pair_got.at[r, i], at_z(2 * way))

        def third(self):
            r = self.r
            total = piece(part, r, 0)[...]
            for i, way in enumerate((+1, -1)):
                self.cps["near", way].wait_recv()
                total = total + near_got[r, i].astype(F32)
            for i, way in enumerate((+1, -1)):
                self.cps["pair", way].wait_recv()
                total = total + pair_got[r, i].astype(F32)
            own = piece(hgrad, r, 0)
            own[...] = total.astype(BF16)
            for way in (+1, -1):
                self.cps["all2", way] = send(own, own, at_z(2 * way))
            for way in (+1, -1):
                self.cps["all1", way] = send(own, own, at_z(way))

        def fourth(self):
            r = self.r
            for way in (+1, -1):
                self.cps["all2", way].wait_recv()
                got = piece(hgrad, r, -2 * way)
                self.cps["all3", way] = send(got, got, at_z(way))
                got = piece(hgrad, r, -2 * way, halves[way])
                self.cps["all4", way] = send(got, got, at_z(2 * way))

        def last(self):
            for way in (+1, -1):
                for name in ("all1", "all3", "all4"):
                    self.cps[name, way].wait_recv()

    def partial_sums(r):
        left = cot[r].reshape(CHUNK, D_CHIP)
        for n in (0, 1):
            cols = pl.ds(n * 256, 256)
            value = nt_dot(left, wd[cols, :]).reshape(2, 2 * TOK, 256)
            part[r, :, :, cols] = value
            part16[r, :, :, cols] = value.astype(BF16)

    def activations(r):
        @pl.loop(0, 4)
        def _(i):
            rows = pl.ds(pl.multiple_of((i % 2) * TOK, TOK), TOK)
            g = gate[r, i // 2, rows].astype(F32)
            u = up[r, i // 2, rows].astype(F32)
            s = 1.0 / (1.0 + jnp.exp(-g))
            silu = g * s
            hidden[r, i // 2, rows] = (silu * u).astype(BF16)
            lin_g[r, i // 2, rows] = u * s * (1.0 + g * (1.0 - s))
            lin_u[r, i // 2, rows] = silu

    def deltas(r):
        @pl.loop(0, 4)
        def _(i):
            rows = pl.ds(pl.multiple_of((i % 2) * TOK, TOK), TOK)
            hg = hgrad[r, i // 2, rows].astype(F32)
            delta_g[r, i // 2, rows] = (hg * lin_g[r, i // 2, rows]).astype(BF16)
            delta_u[r, i // 2, rows] = (hg * lin_u[r, i // 2, rows]).astype(BF16)

    def input_part(r):
        left_g = delta_g[r].reshape(CHUNK, F_OWN)
        left_u = delta_u[r].reshape(CHUNK, F_OWN)
        for i in range(D_CHIP // 256):
            n = pl.ds(i * 256, 256)
            term = nt_dot(left_g, wg[n, :]) + nt_dot(left_u, wu[n, :])
            term = term.reshape(2, 2 * TOK, 256)
            if r == 0:
                ig_mine[:, :, n] = term
            else:
                xs_send[r - 1, :, :, n] = term.astype(BF16)

    xs_cps = {}

    def send_x(r):
        dx = {1: 1, 2: 3}[r]
        for k in (0, 1):
            xs_cps[r, k] = send(xs_send.at[r - 1, k], xs_got.at[r - 1, k], at_x(dx))

    def sum_x(k):
        total = ig_mine[k]
        for r in (1, 2):
            xs_cps[r, k].wait_recv()
            total = total + xs_got[r - 1, k].astype(F32)
        ys_send[k] = total.astype(BF16)

    def send_y(src, k, got, sems):
        for h in (0, 1):
            yy = 4 * k + 2 * core + h
            rows = pl.ds(h * TOK, TOK)

            def copy(q, cols, on_core, rows=rows, yy=yy):
                return pltpu.make_async_remote_copy(
                    src_ref=src.at[k, rows, cols], dst_ref=got.at[y],
                    send_sem=send_sems.at[q], recv_sem=sems.at[y],
                    device_id=(z * 2 + on_core, x * N_Y + yy), device_id_type=MESH,
                )

            cp = copy(len(copies), hi, 1 - core)
            cp.start()
            copies.append(cp)
            q = N_SEMS - 1 - len(late_sends)
            late_sends.append((lambda q=q, copy=copy: copy(q, lo, core), yy != y))

            @pl.when(yy != y)
            def _(q=q, copy=copy):
                copy(q, lo, core).start()

            @pl.when(yy == y)
            def _(rows=rows):
                pltpu.make_async_copy(src.at[k, rows, lo], got.at[y], sems.at[y]).start()

    def sum_y(got, sems):
        total = jnp.zeros((TOK, D_OWN), F32)
        for yy in range(N_Y):
            dst = got.at[yy]
            pltpu.make_async_copy(dst, dst, sems.at[yy]).wait()
            total = total + got[yy].astype(F32)
        return total

    def flat(buf, first, count, width):
        return buf.at[pl.ds(first, count)].reshape(count * CHUNK, width)

    def down_grad():
        left = flat(hidden, 0, 4, F_OWN)
        right = flat(cot, 0, 4, D_CHIP)

        @pl.loop(0, F_OWN // 128)
        def _(i):
            rows = pl.ds(pl.multiple_of(i * 128, 128), 128)
            both = tn_dot(left[:, rows], right[...])
            dg_own[rows, :] = both[:, :D_OWN]
            dg_send[rows, :] = both[:, D_OWN:].astype(BF16)

        return send(dg_send, dg_got, sib)

    def weight_grad(delta, own, first, count, sent=None):
        left = flat(inp, first, count, D_CHIP)
        right = flat(delta, first, count, F_OWN)

        @pl.loop(0, D_CHIP // 128)
        def _(i):
            rows = pl.ds(pl.multiple_of(i * 128, 128), 128)
            value = tn_dot(left[:, rows], right[...])
            if first > 0:
                value = value + own[rows, :]
            own[rows, :] = value

        if sent is not None:
            sent[...] = own[hi, :].astype(BF16)

    def finish(own, got, cp, out):
        cp.wait_recv()
        out[...] = (own[pl.ds(0, out.shape[0]), :] + got[...].astype(F32)).astype(BF16)

    cot_far_cp = send(cot_in, cot_far, at_x(2))
    over_y(cot_in, cot, 0, cot_sems)
    rings = [
        Ring(gate, gate_in, +1, 0), Ring(up, up_in, -1, 0),
        Ring(gate, gate_in, -1, 1), Ring(up, up_in, +1, 1),
    ]
    for ring in rings:
        ring.start(1)
    wd_self.wait()
    wd_cp = send(wd.at[:, lo], wd.at[:, hi], sib)
    gate_self = move(gate_in, gate.at[chunk_of(z // 2), z % 2])
    up_self = move(up_in, up.at[chunk_of(z // 2), z % 2])

    sums = [SumOverZ(r) for r in range(4)]
    rings[0].step(1)
    rings[1].step(1)
    over_y_wait(cot, 0, cot_sems, k_near)
    cot_far_cp.wait_recv()
    over_y(cot_far, cot, 3, cot_far_sems)
    cot_cps = [over_x(cot, k_near)]
    rings[2].step(1)
    rings[3].step(1)
    rings[0].step(2)
    over_y_wait(cot, 0, cot_sems, 1 - k_near)
    cot_cps.append(over_x(cot, 1 - k_near))
    rings[1].step(2)
    inp_far_cp = send(inp_in, inp_far, at_x(2))
    rings[2].step(2)
    wd_cp.wait_recv()
    partial_sums(0)
    sums[0].first()
    rings[3].step(2)
    wg_self.wait()
    wg_cp = send(wg.at[lo], wg.at[hi], sib)
    wu_self.wait()
    wu_cp = send(wu.at[lo], wu.at[hi], sib)
    rings[0].step(3)
    rings[1].step(3)
    rings[2].step(3)
    sums[0].second()
    rings[3].step(3)
    for r in (2, 1):
        over_x_wait(cot_cps, r)
        partial_sums(r)
        sums[r].first()
    for k in (0, 1):
        over_y_wait(cot, 3, cot_far_sems, k)
    partial_sums(3)
    sums[3].first()
    over_y(inp_in, inp, 0, inp_sems)
    inp_far_cp.wait_recv()
    over_y(inp_far, inp, 3, inp_far_sems)
    sums[0].third()
    sums[2].second()
    sums[1].second()
    sums[3].second()
    inp_cps = []
    for k in (0, 1):
        over_y_wait(inp, 0, inp_sems, k)
        inp_cps.append(over_x(inp, k))
    sums[0].fourth()
    sums[2].third()
    sums[1].third()
    sums[3].third()
    for ring in rings:
        ring.wait(4)
    gate_self.wait()
    up_self.wait()
    activations(0)
    activations(2)
    wg_cp.wait_recv()
    wu_cp.wait_recv()
    sums[2].fourth()
    sums[1].fourth()
    sums[3].fourth()
    activations(1)
    activations(3)
    sums[0].last()
    deltas(0)
    input_part(0)
    for r in (2, 1):
        sums[r].last()
        deltas(r)
        input_part(r)
        send_x(r)
    sums[3].last()
    deltas(3)
    input_part(3)
    for k in (0, 1):
        send_y(xs_send.at[2], k, yf_got, yf_sems)
    dg_cp = down_grad()
    for k in (0, 1):
        sum_x(k)
        send_y(ys_send, k, ys_got, ys_sems)
    for k in (0, 1):
        over_y_wait(inp, 3, inp_far_sems, k)
    for r in (1, 2):
        over_x_wait(inp_cps, r)
    weight_grad(delta_g, gg_own, 0, 4, gg_send)
    gg_cp = send(gg_send, gg_got, sib)
    far_sum[...] = sum_y(yf_got, yf_sems).astype(BF16)
    far_cp = send(far_sum, far_back, at_x(2))
    weight_grad(delta_u, ug_own, 0, 4, ug_send)
    ug_cp = send(ug_send, ug_got, sib)
    finish(dg_own, dg_got, dg_cp, dg_out)
    finish(gg_own, gg_got, gg_cp, gg_out)
    finish(ug_own, ug_got, ug_cp, ug_out)
    for cp in copies:
        cp.wait_send()
    for make, remote in late_sends:
        @pl.when(remote)
        def _(make=make):
            make().wait_send()

    total = sum_y(ys_got, ys_sems)
    far_cp.wait_recv()
    ig_out[...] = (total + far_back[...].astype(F32)).astype(BF16)


def copy_kernel(a, b, c, d, a_out, b_out, c_out, d_out, sems):
    pairs = ((a, a_out), (b, b_out), (c, c_out), (d, d_out))
    cps = [pltpu.make_async_copy(src, dst, sems.at[i]) for i, (src, dst) in enumerate(pairs)]
    for cp in cps:
        cp.start()
    for cp in cps:
        cp.wait()


def on_device(inputs, cotangent, gate_pre, up_pre, gate_weight, up_weight, down_weight):
    vmem = pl.BlockSpec(memory_space=pltpu.VMEM)
    hbm = pl.BlockSpec(memory_space=pl.ANY)
    shape = jax.ShapeDtypeStruct
    outs = (
        shape((TOK, D_OWN), BF16),
        shape((D_OWN, F_OWN), BF16),
        shape((D_OWN, F_OWN), BF16),
        shape((F_OWN, D_OWN), BF16),
    )
    by_token = lambda width, kind: pltpu.VMEM((4, 2, 2 * TOK, width), kind)
    z_piece = pltpu.VMEM((4, 2, 2 * TOK, F_PART), BF16)
    scratch = [
        pltpu.VMEM((4, 2, 2, TOK, D_CHIP), BF16),
        pltpu.VMEM((4, 2, 2, TOK, D_CHIP), BF16),
        by_token(F_OWN, BF16),
        by_token(F_OWN, BF16),
        pltpu.VMEM((D_CHIP, F_OWN), BF16),
        pltpu.VMEM((D_CHIP, F_OWN), BF16),
        pltpu.VMEM((F_OWN, D_CHIP), BF16),
        by_token(F_OWN, F32),
        by_token(F_OWN, BF16),
        z_piece,
        z_piece,
        pltpu.VMEM((4, 2, TOK, F_PART), BF16),
        z_piece,
        z_piece,
        by_token(F_OWN, BF16),
        by_token(F_OWN, F32),
        by_token(F_OWN, F32),
        by_token(F_OWN, BF16),
        by_token(F_OWN, BF16),
        by_token(F_OWN, BF16),
        pltpu.VMEM((2, 2 * TOK, D_CHIP), F32),
        pltpu.VMEM((3, 2, 2 * TOK, D_CHIP), BF16),
        pltpu.VMEM((2, 2, 2 * TOK, D_CHIP), BF16),
        pltpu.VMEM((2, 2 * TOK, D_CHIP), BF16),
        pltpu.VMEM((N_Y, TOK, D_OWN), BF16),
        pltpu.VMEM((F_OWN, D_OWN), BF16),
        pltpu.VMEM((D_OWN, F_OWN), BF16),
        pltpu.VMEM((D_OWN, F_OWN), BF16),
        pltpu.VMEM((F_OWN, D_OWN), BF16),
        pltpu.VMEM((D_OWN, F_OWN), BF16),
        pltpu.VMEM((D_OWN, F_OWN), BF16),
        pltpu.VMEM((F_OWN, D_OWN), F32),
        pltpu.VMEM((D_CHIP, F_OWN), F32),
        pltpu.VMEM((D_CHIP, F_OWN), F32),
        pltpu.VMEM((TOK, D_OWN), BF16),
        pltpu.VMEM((TOK, D_OWN), BF16),
        pltpu.VMEM((N_Y, TOK, D_OWN), BF16),
        pltpu.VMEM((TOK, D_OWN), BF16),
        pltpu.VMEM((TOK, D_OWN), BF16),
        pltpu.SemaphoreType.DMA((N_SEMS,)),
        pltpu.SemaphoreType.DMA((N_SEMS,)),
        pltpu.SemaphoreType.DMA((16,)),
    ] + [pltpu.SemaphoreType.DMA((8,))] * 6
    grads = pl.pallas_call(
        kernel,
        out_shape=tuple(pltpu.VMEM(out.shape, out.dtype) for out in outs),
        in_specs=[vmem] * 4 + [hbm] * 3,
        out_specs=(vmem,) * 4,
        scratch_shapes=scratch,
        compiler_params=pltpu.CompilerParams(
            collective_id=0, has_side_effects=True, vmem_limit_bytes=56 * 1024 * 1024
        ),
        cost_estimate=pl.CostEstimate(
            flops=3_700_000_000, bytes_accessed=3_000_000, transcendentals=400_000
        ),
    )(inputs, cotangent, gate_pre, up_pre, gate_weight, up_weight, down_weight)
    return pl.pallas_call(
        copy_kernel,
        out_shape=outs,
        in_specs=[vmem] * 4,
        out_specs=(hbm,) * 4,
        scratch_shapes=[pltpu.SemaphoreType.DMA((4,))],
    )(*[pltpu.with_memory_space_constraint(g, pltpu.VMEM) for g in grads])


def solution(mesh):
    placed = (
        P("col", "row"),
        P("col", "row"),
        P("row", "col"),
        P("row", "col"),
        P("row", "col"),
        P("row", "col"),
        P("col", "row"),
    )
    return jax.shard_map(
        on_device,
        mesh=mesh,
        in_specs=placed,
        out_specs=(P("col", "row"), P("row", "col"), P("row", "col"), P("col", "row")),
        check_vma=False,
    )
```

```python
import jax
import jax.numpy as jnp
from jax import lax
from jax.experimental import pallas as pl
from jax.experimental.pallas import tpu as pltpu
from jax.sharding import PartitionSpec as P

MESH = pl.DeviceIdType.MESH
BF16 = jnp.bfloat16
F32 = jnp.float32

N_X, N_Y, N_Z = 4, 8, 8
TOK = 48
D_OWN = 384
D_CHIP = 768
F_OWN = 512
CHUNK = 192
F_PART = 128
N_SEMS = 220


def nt_dot(left, right):
    return lax.dot_general(left, right, (((1,), (1,)), ((), ())), preferred_element_type=F32)


def tn_dot(left, right):
    return lax.dot_general(left, right, (((0,), (0,)), ((), ())), preferred_element_type=F32)


def kernel(
    inp_in, cot_in, gate_in, up_in, wg_in, wu_in, wd_in,
    ig_out, gg_out, ug_out, dg_out,
    cot, inp, gate, up, wg, wu, wd,
    part, part16, near_got, far_got, half_got, pair_got, pair_send, hgrad,
    lin_g, lin_u, hidden, delta_g, delta_u,
    ig_mine, xs_send, xs_got, ys_send, ys_got,
    dg_send, gg_send, ug_send, dg_got, gg_got, ug_got, dg_own, gg_own, ug_own,
    cot_far, inp_far, yf_got, far_sum, far_back,
    send_sems, recv_sems, local_sems, cot_sems, inp_sems, ys_sems,
    cot_far_sems, inp_far_sems, yf_sems,
):
    row = lax.axis_index("row")
    col = lax.axis_index("col")
    z, core = row // 2, row % 2
    x, y = col // N_Y, col % N_Y

    def at_z(dz):
        return (((z + dz + N_Z) % N_Z) * 2 + core, col)

    def at_x(dx):
        return (row, ((x + dx + N_X) % N_X) * N_Y + y)

    def at_y(dy, on_core):
        return (z * 2 + on_core, x * N_Y + (y + dy) % N_Y)

    sib = at_y(0, 1 - core)

    copies = []
    local = []

    def send(src, dst, device):
        k = len(copies)
        cp = pltpu.make_async_remote_copy(
            src_ref=src, dst_ref=dst, send_sem=send_sems.at[k], recv_sem=recv_sems.at[k],
            device_id=device, device_id_type=MESH,
        )
        cp.start()
        copies.append(cp)
        return cp

    def move(src, dst):
        cp = pltpu.make_async_copy(src, dst, local_sems.at[len(local)])
        cp.start()
        local.append(cp)
        return cp

    lo, hi = pl.ds(0, D_OWN), pl.ds(D_OWN, D_OWN)

    wd_self = move(wd_in, wd.at[:, lo])
    wg_self = move(wg_in, wg.at[lo])
    wu_self = move(wu_in, wu.at[lo])

    barrier = pltpu.get_barrier_semaphore()
    others = [sib] + [at_y(dy, c) for dy in range(1, N_Y) for c in (0, 1)]
    others += [at_x(dx) for dx in (1, 2, 3)] + [at_z(dz) for dz in (1, 2, 6, 7)]
    for dev in others:
        pl.semaphore_signal(barrier, inc=1, device_id=dev, device_id_type=MESH)
    pl.semaphore_wait(barrier, len(others))

    def chunk_of(xx):
        dx = (xx - x + N_X) % N_X
        return dx + (dx // 2) * (5 - 2 * dx)

    c_y, k_y, h_y = (y // 2) % 2, y // 4, y % 2
    side = (core + c_y) % 2
    y_sem = (k_y * 2 + h_y) * 2 + side
    late_sends = []

    def over_y(src, buf, r, sems):
        dst = buf.at[r, k_y, h_y, :, pl.ds(pl.multiple_of(side * D_OWN, 128), D_OWN)]

        def copy(k, device):
            return pltpu.make_async_remote_copy(
                src_ref=src, dst_ref=dst, send_sem=send_sems.at[k], recv_sem=sems.at[y_sem],
                device_id=device, device_id_type=MESH,
            )

        for dy in (1, 7, 2, 6, 3, 5, 4):
            cp = copy(len(copies), at_y(dy, c_y))
            cp.start()
            copies.append(cp)
        k = N_SEMS - 1 - len(late_sends)
        late_sends.append((lambda: copy(k, sib), side == 1))

        @pl.when(side == 0)
        def _():
            pltpu.make_async_copy(src, dst, sems.at[y_sem]).start()

        @pl.when(side == 1)
        def _():
            copy(k, sib).start()

    def over_y_wait(buf, r, sems, k):
        for h in (0, 1):
            for s, cols in ((0, lo), (1, hi)):
                dst = buf.at[r, k, h, :, cols]
                pltpu.make_async_copy(dst, dst, sems.at[(k * 2 + h) * 2 + s]).wait()

    k_near = (((y - 2 * core + N_Y) % N_Y + 1) // 4) % 2

    def over_x(buf, k):
        return {
            r: send(buf.at[0, k], buf.at[r, k], at_x(dx)) for dx, r in ((1, 2), (3, 1))
        }

    def over_x_wait(parts, r):
        for cps in parts:
            cps[r].wait_recv()

    class Ring:
        def __init__(self, buf, own, long_way, h):
            self.rows = pl.ds(h * TOK, TOK)
            self.buf, self.own = buf, own.at[self.rows]
            self.hops = {long_way: N_Z // 2, -long_way: N_Z // 2 - 1}
            self.cps = {}

        def slot(self, zz):
            return self.buf.at[chunk_of(zz // 2), zz % 2, self.rows]

        def start(self, s):
            for way in (+1, -1):
                if s <= self.hops[way]:
                    owner = (z - way * (s - 1) + N_Z) % N_Z
                    src = self.own if s == 1 else self.slot(owner)
                    self.cps[way, s] = send(src, self.slot(owner), at_z(way))

        def wait(self, s):
            for way in (+1, -1):
                if s <= self.hops[way]:
                    self.cps[way, s].wait_recv()

        def step(self, s):
            self.wait(s)
            self.start(s + 1)

    def piece(buf, r, dz, rows=pl.ds(0, 2 * TOK)):
        o = (z + dz + N_Z) % N_Z
        return buf.at[r, o // 4, rows, pl.ds(pl.multiple_of((o % 4) * F_PART, F_PART), F_PART)]

    halves = {+1: pl.ds(0, TOK), -1: pl.ds(TOK, TOK)}

    class SumOverZ:
        def __init__(self, r):
            self.r = r
            self.cps = {}

        def first(self):
            r = self.r
            for i, way in enumerate((+1, -1)):
                self.cps["far", way] = send(piece(part16, r, 3 * way), far_got.at[r, i], at_z(way))
                self.cps["half", way] = send(
                    piece(part16, r, 4, halves[way]), half_got.at[r, i], at_z(2 * way)
                )
            for i, way in enumerate((+1, -1)):
                self.cps["near", way] = send(piece(part16, r, way), near_got.at[r, i], at_z(way))

        def second(self):
            r = self.r
            for i, way in enumerate((+1, -1)):
                self.cps["far", way].wait_recv()
                self.cps["half", way].wait_recv()
                total = piece(part, r, 2 * way)[...] + far_got[r, i].astype(F32)
                extra = half_got[r, i].astype(F32)
                rest = jnp.zeros_like(extra)
                rows = (extra, rest) if way == 1 else (rest, extra)
                pair_send[r, i] = (total + jnp.concatenate(rows, axis=0)).astype(BF16)
                self.cps["pair", way] = send(pair_send.at[r, i], pair_got.at[r, i], at_z(2 * way))

        def third(self):
            r = self.r
            total = piece(part, r, 0)[...]
            for i, way in enumerate((+1, -1)):
                self.cps["near", way].wait_recv()
                total = total + near_got[r, i].astype(F32)
            for i, way in enumerate((+1, -1)):
                self.cps["pair", way].wait_recv()
                total = total + pair_got[r, i].astype(F32)
            own = piece(hgrad, r, 0)
            own[...] = total.astype(BF16)
            for way in (+1, -1):
                self.cps["all2", way] = send(own, own, at_z(2 * way))
            for way in (+1, -1):
                self.cps["all1", way] = send(own, own, at_z(way))

        def fourth(self):
            r = self.r
            for way in (+1, -1):
                self.cps["all2", way].wait_recv()
                got = piece(hgrad, r, -2 * way)
                self.cps["all3", way] = send(got, got, at_z(way))
                got = piece(hgrad, r, -2 * way, halves[way])
                self.cps["all4", way] = send(got, got, at_z(2 * way))

        def last(self):
            for way in (+1, -1):
                for name in ("all1", "all3", "all4"):
                    self.cps[name, way].wait_recv()

    def partial_sums(r):
        left = cot[r].reshape(CHUNK, D_CHIP)
        for n in (0, 1):
            cols = pl.ds(n * 256, 256)
            value = nt_dot(left, wd[cols, :]).reshape(2, 2 * TOK, 256)
            part[r, :, :, cols] = value
            part16[r, :, :, cols] = value.astype(BF16)

    def activations(r):
        @pl.loop(0, 4)
        def _(i):
            rows = pl.ds(pl.multiple_of((i % 2) * TOK, TOK), TOK)
            g = gate[r, i // 2, rows].astype(F32)
            u = up[r, i // 2, rows].astype(F32)
            s = 1.0 / (1.0 + jnp.exp(-g))
            silu = g * s
            hidden[r, i // 2, rows] = (silu * u).astype(BF16)
            lin_g[r, i // 2, rows] = u * s * (1.0 + g * (1.0 - s))
            lin_u[r, i // 2, rows] = silu

    def deltas(r):
        @pl.loop(0, 4)
        def _(i):
            rows = pl.ds(pl.multiple_of((i % 2) * TOK, TOK), TOK)
            hg = hgrad[r, i // 2, rows].astype(F32)
            delta_g[r, i // 2, rows] = (hg * lin_g[r, i // 2, rows]).astype(BF16)
            delta_u[r, i // 2, rows] = (hg * lin_u[r, i // 2, rows]).astype(BF16)

    def input_part(r):
        left_g = delta_g[r].reshape(CHUNK, F_OWN)
        left_u = delta_u[r].reshape(CHUNK, F_OWN)
        for i in range(D_CHIP // 256):
            n = pl.ds(i * 256, 256)
            term = nt_dot(left_g, wg[n, :]) + nt_dot(left_u, wu[n, :])
            term = term.reshape(2, 2 * TOK, 256)
            if r == 0:
                ig_mine[:, :, n] = term
            else:
                xs_send[r - 1, :, :, n] = term.astype(BF16)

    xs_cps = {}

    def send_x(r):
        dx = {1: 1, 2: 3}[r]
        for k in (0, 1):
            xs_cps[r, k] = send(xs_send.at[r - 1, k], xs_got.at[r - 1, k], at_x(dx))

    def sum_x(k):
        total = ig_mine[k]
        for r in (1, 2):
            xs_cps[r, k].wait_recv()
            total = total + xs_got[r - 1, k].astype(F32)
        ys_send[k] = total.astype(BF16)

    def send_y(src, k, got, sems):
        for h in (0, 1):
            yy = 4 * k + 2 * core + h
            rows = pl.ds(h * TOK, TOK)

            def copy(q, cols, on_core, rows=rows, yy=yy):
                return pltpu.make_async_remote_copy(
                    src_ref=src.at[k, rows, cols], dst_ref=got.at[y],
                    send_sem=send_sems.at[q], recv_sem=sems.at[y],
                    device_id=(z * 2 + on_core, x * N_Y + yy), device_id_type=MESH,
                )

            cp = copy(len(copies), hi, 1 - core)
            cp.start()
            copies.append(cp)
            q = N_SEMS - 1 - len(late_sends)
            late_sends.append((lambda q=q, copy=copy: copy(q, lo, core), yy != y))

            @pl.when(yy != y)
            def _(q=q, copy=copy):
                copy(q, lo, core).start()

            @pl.when(yy == y)
            def _(rows=rows):
                pltpu.make_async_copy(src.at[k, rows, lo], got.at[y], sems.at[y]).start()

    def sum_y(got, sems):
        total = jnp.zeros((TOK, D_OWN), F32)
        for yy in range(N_Y):
            dst = got.at[yy]
            pltpu.make_async_copy(dst, dst, sems.at[yy]).wait()
            total = total + got[yy].astype(F32)
        return total

    def flat(buf, first, count, width):
        return buf.at[pl.ds(first, count)].reshape(count * CHUNK, width)

    def down_grad():
        left = flat(hidden, 0, 4, F_OWN)
        right = flat(cot, 0, 4, D_CHIP)

        @pl.loop(0, F_OWN // 128)
        def _(i):
            rows = pl.ds(pl.multiple_of(i * 128, 128), 128)
            both = tn_dot(left[:, rows], right[...])
            dg_own[rows, :] = both[:, :D_OWN]
            dg_send[rows, :] = both[:, D_OWN:].astype(BF16)

        return send(dg_send, dg_got, sib)

    def weight_grad(delta, own, first, count, sent=None):
        left = flat(inp, first, count, D_CHIP)
        right = flat(delta, first, count, F_OWN)

        @pl.loop(0, D_CHIP // 128)
        def _(i):
            rows = pl.ds(pl.multiple_of(i * 128, 128), 128)
            value = tn_dot(left[:, rows], right[...])
            if first > 0:
                value = value + own[rows, :]
            own[rows, :] = value

        if sent is not None:
            sent[...] = own[hi, :].astype(BF16)

    def finish(own, got, cp, out):
        cp.wait_recv()
        out[...] = (own[pl.ds(0, out.shape[0]), :] + got[...].astype(F32)).astype(BF16)

    cot_far_cp = send(cot_in, cot_far, at_x(2))
    over_y(cot_in, cot, 0, cot_sems)
    rings = [
        Ring(gate, gate_in, +1, 0), Ring(up, up_in, -1, 0),
        Ring(gate, gate_in, -1, 1), Ring(up, up_in, +1, 1),
    ]
    for ring in rings:
        ring.start(1)
    wd_self.wait()
    wd_cp = send(wd.at[:, lo], wd.at[:, hi], sib)
    gate_self = move(gate_in, gate.at[chunk_of(z // 2), z % 2])
    up_self = move(up_in, up.at[chunk_of(z // 2), z % 2])

    sums = [SumOverZ(r) for r in range(4)]
    rings[0].step(1)
    rings[1].step(1)
    over_y_wait(cot, 0, cot_sems, k_near)
    cot_far_cp.wait_recv()
    over_y(cot_far, cot, 3, cot_far_sems)
    cot_cps = [over_x(cot, k_near)]
    rings[2].step(1)
    rings[3].step(1)
    rings[0].step(2)
    over_y_wait(cot, 0, cot_sems, 1 - k_near)
    cot_cps.append(over_x(cot, 1 - k_near))
    rings[1].step(2)
    inp_far_cp = send(inp_in, inp_far, at_x(2))
    rings[2].step(2)
    wd_cp.wait_recv()
    partial_sums(0)
    sums[0].first()
    rings[3].step(2)
    wg_self.wait()
    wg_cp = send(wg.at[lo], wg.at[hi], sib)
    wu_self.wait()
    wu_cp = send(wu.at[lo], wu.at[hi], sib)
    rings[0].step(3)
    rings[1].step(3)
    rings[2].step(3)
    sums[0].second()
    rings[3].step(3)
    for k in (0, 1):
        over_y_wait(cot, 3, cot_far_sems, k)
    partial_sums(3)
    sums[3].first()
    for r in (2, 1):
        over_x_wait(cot_cps, r)
        partial_sums(r)
        sums[r].first()
    over_y(inp_in, inp, 0, inp_sems)
    inp_far_cp.wait_recv()
    over_y(inp_far, inp, 3, inp_far_sems)
    sums[0].third()
    sums[2].second()
    sums[1].second()
    sums[3].second()
    inp_cps = []
    for k in (0, 1):
        over_y_wait(inp, 0, inp_sems, k)
        inp_cps.append(over_x(inp, k))
    sums[0].fourth()
    sums[2].third()
    sums[1].third()
    sums[3].third()
    wg_cp.wait_recv()
    wu_cp.wait_recv()
    sums[2].fourth()
    sums[1].fourth()
    sums[3].fourth()
    for ring in rings:
        ring.wait(4)
    gate_self.wait()
    up_self.wait()
    activations(0)
    activations(2)
    activations(1)
    activations(3)
    sums[0].last()
    deltas(0)
    input_part(0)
    for r in (2, 1):
        sums[r].last()
        deltas(r)
        input_part(r)
        send_x(r)
    sums[3].last()
    deltas(3)
    input_part(3)
    for k in (0, 1):
        send_y(xs_send.at[2], k, yf_got, yf_sems)
    dg_cp = down_grad()
    for k in (0, 1):
        sum_x(k)
        send_y(ys_send, k, ys_got, ys_sems)
    for k in (0, 1):
        over_y_wait(inp, 3, inp_far_sems, k)
    for r in (1, 2):
        over_x_wait(inp_cps, r)
    weight_grad(delta_g, gg_own, 0, 4, gg_send)
    gg_cp = send(gg_send, gg_got, sib)
    far_sum[...] = sum_y(yf_got, yf_sems).astype(BF16)
    far_cp = send(far_sum, far_back, at_x(2))
    weight_grad(delta_u, ug_own, 0, 4, ug_send)
    ug_cp = send(ug_send, ug_got, sib)
    finish(dg_own, dg_got, dg_cp, dg_out)
    finish(gg_own, gg_got, gg_cp, gg_out)
    finish(ug_own, ug_got, ug_cp, ug_out)
    for cp in copies:
        cp.wait_send()
    for make, remote in late_sends:
        @pl.when(remote)
        def _(make=make):
            make().wait_send()

    total = sum_y(ys_got, ys_sems)
    far_cp.wait_recv()
    ig_out[...] = (total + far_back[...].astype(F32)).astype(BF16)


def copy_kernel(a, b, c, d, a_out, b_out, c_out, d_out, sems):
    pairs = ((a, a_out), (b, b_out), (c, c_out), (d, d_out))
    cps = [pltpu.make_async_copy(src, dst, sems.at[i]) for i, (src, dst) in enumerate(pairs)]
    for cp in cps:
        cp.start()
    for cp in cps:
        cp.wait()


def on_device(inputs, cotangent, gate_pre, up_pre, gate_weight, up_weight, down_weight):
    vmem = pl.BlockSpec(memory_space=pltpu.VMEM)
    hbm = pl.BlockSpec(memory_space=pl.ANY)
    shape = jax.ShapeDtypeStruct
    outs = (
        shape((TOK, D_OWN), BF16),
        shape((D_OWN, F_OWN), BF16),
        shape((D_OWN, F_OWN), BF16),
        shape((F_OWN, D_OWN), BF16),
    )
    by_token = lambda width, kind: pltpu.VMEM((4, 2, 2 * TOK, width), kind)
    z_piece = pltpu.VMEM((4, 2, 2 * TOK, F_PART), BF16)
    scratch = [
        pltpu.VMEM((4, 2, 2, TOK, D_CHIP), BF16),
        pltpu.VMEM((4, 2, 2, TOK, D_CHIP), BF16),
        by_token(F_OWN, BF16),
        by_token(F_OWN, BF16),
        pltpu.VMEM((D_CHIP, F_OWN), BF16),
        pltpu.VMEM((D_CHIP, F_OWN), BF16),
        pltpu.VMEM((F_OWN, D_CHIP), BF16),
        by_token(F_OWN, F32),
        by_token(F_OWN, BF16),
        z_piece,
        z_piece,
        pltpu.VMEM((4, 2, TOK, F_PART), BF16),
        z_piece,
        z_piece,
        by_token(F_OWN, BF16),
        by_token(F_OWN, F32),
        by_token(F_OWN, F32),
        by_token(F_OWN, BF16),
        by_token(F_OWN, BF16),
        by_token(F_OWN, BF16),
        pltpu.VMEM((2, 2 * TOK, D_CHIP), F32),
        pltpu.VMEM((3, 2, 2 * TOK, D_CHIP), BF16),
        pltpu.VMEM((2, 2, 2 * TOK, D_CHIP), BF16),
        pltpu.VMEM((2, 2 * TOK, D_CHIP), BF16),
        pltpu.VMEM((N_Y, TOK, D_OWN), BF16),
        pltpu.VMEM((F_OWN, D_OWN), BF16),
        pltpu.VMEM((D_OWN, F_OWN), BF16),
        pltpu.VMEM((D_OWN, F_OWN), BF16),
        pltpu.VMEM((F_OWN, D_OWN), BF16),
        pltpu.VMEM((D_OWN, F_OWN), BF16),
        pltpu.VMEM((D_OWN, F_OWN), BF16),
        pltpu.VMEM((F_OWN, D_OWN), F32),
        pltpu.VMEM((D_CHIP, F_OWN), F32),
        pltpu.VMEM((D_CHIP, F_OWN), F32),
        pltpu.VMEM((TOK, D_OWN), BF16),
        pltpu.VMEM((TOK, D_OWN), BF16),
        pltpu.VMEM((N_Y, TOK, D_OWN), BF16),
        pltpu.VMEM((TOK, D_OWN), BF16),
        pltpu.VMEM((TOK, D_OWN), BF16),
        pltpu.SemaphoreType.DMA((N_SEMS,)),
        pltpu.SemaphoreType.DMA((N_SEMS,)),
        pltpu.SemaphoreType.DMA((16,)),
    ] + [pltpu.SemaphoreType.DMA((8,))] * 6
    grads = pl.pallas_call(
        kernel,
        out_shape=tuple(pltpu.VMEM(out.shape, out.dtype) for out in outs),
        in_specs=[vmem] * 4 + [hbm] * 3,
        out_specs=(vmem,) * 4,
        scratch_shapes=scratch,
        compiler_params=pltpu.CompilerParams(
            collective_id=0, has_side_effects=True, vmem_limit_bytes=56 * 1024 * 1024
        ),
        cost_estimate=pl.CostEstimate(
            flops=3_700_000_000, bytes_accessed=3_000_000, transcendentals=400_000
        ),
    )(inputs, cotangent, gate_pre, up_pre, gate_weight, up_weight, down_weight)
    return pl.pallas_call(
        copy_kernel,
        out_shape=outs,
        in_specs=[vmem] * 4,
        out_specs=(hbm,) * 4,
        scratch_shapes=[pltpu.SemaphoreType.DMA((4,))],
    )(*[pltpu.with_memory_space_constraint(g, pltpu.VMEM) for g in grads])


def solution(mesh):
    placed = (
        P("col", "row"),
        P("col", "row"),
        P("row", "col"),
        P("row", "col"),
        P("row", "col"),
        P("row", "col"),
        P("col", "row"),
    )
    return jax.shard_map(
        on_device,
        mesh=mesh,
        in_specs=placed,
        out_specs=(P("col", "row"), P("row", "col"), P("row", "col"), P("col", "row")),
        check_vma=False,
    )
```
